128 devices in a mesh: row: 8 (over x_hi, z), col: 16 (over x_lo, y, core).
Axes of the slice: x: 4 (x_hi: 2, x_lo: 2; x = x_hi * 2 + x_lo), y: 4, z: 4, core: 2. Of those that a mesh axis runs over, the one named last changes fastest.
Arguments:
- pair: bfloat16 [512, 512, 128], P('row', 'col'), may hold values from -6 to 6
- cotangent: bfloat16 [512, 512, 128], P('row', 'col'), may hold values from -6 to 6
- in_gain: float32 [128], replicated, may hold values from 0.5 to 1.5
- w_in: bfloat16 [128, 640], replicated, may hold values from -0.5 to 0.5
- out_gain: float32 [128], replicated, may hold values from 0.5 to 1.5
- w_out: bfloat16 [128, 128], replicated, may hold values from -0.5 to 0.5
Outputs:
- pair_next: bfloat16 [512, 512, 128], P('row', 'col')
- pair_back: bfloat16 [512, 512, 128], P('row', 'col')
- in_gain_grad: float32 [128], replicated
- w_in_grad: float32 [128, 640], replicated
- out_gain_grad: float32 [128], replicated
- w_out_grad: float32 [128, 128], replicated
The draws below stay inside these ranges and needn't reach their ends.
All inputs are finite; a program needn't handle non-finite values.
Results may differ from the reference program's by a relative error of at most 0.0081.
Values may be sent and summed in bfloat16 or wider, within the bound.
A program may use at most 128 MiB of HBM per device.

```python
import jax
import jax.numpy as jnp
from jax import lax

PAIR_CH = 128
HIDDEN_SIZE = 128
RES = 512


def block_levels(stream_key, dims, split, low, top_value):
    loudness, own = 1.0, jax.random.fold_in(stream_key, 6)
    for position, shards_of in split:
        steps = jnp.exp(jax.random.uniform(jax.random.fold_in(own, position), (shards_of,), jnp.float32, low / len(split), top_value / len(split)))
        loudness = loudness * jnp.repeat(steps, dims[position] // shards_of).reshape([-1 if axis == position else 1 for axis in range(len(dims))])
    return loudness


def bell_draw(own_key, extent, deviation, reach, cuts=(), held_as=jnp.bfloat16):
    result = jax.random.normal(own_key, extent, jnp.float32) * deviation
    if len(cuts) > 0:
        result = block_levels(own_key, extent, cuts, -0.22, 0.18) * result
    return jnp.clip(result, min=-reach, max=reach).astype(held_as)


def setup_inputs(seed: int = 0) -> dict:
    key_list = jax.random.split(jax.random.key(seed), 7)
    pair = bell_draw(key_list[0], (RES, RES, PAIR_CH), 1.0, 6.0, ((0, 8), (1, 16)))
    cotangent = bell_draw(key_list[1], (RES, RES, PAIR_CH), 1.0, 6.0, ((0, 8), (1, 16)))
    in_gain = jnp.clip(1.0 + 0.1 * jax.random.normal(key_list[2], (PAIR_CH,), jnp.float32), 0.5, 1.5)
    w_in = bell_draw(key_list[3], (PAIR_CH, 4 * HIDDEN_SIZE + PAIR_CH), PAIR_CH ** -0.5, 0.5)
    out_gain = jnp.clip(1.0 + 0.1 * jax.random.normal(key_list[4], (HIDDEN_SIZE,), jnp.float32), 0.5, 1.5)
    w_out = bell_draw(key_list[5], (HIDDEN_SIZE, PAIR_CH), HIDDEN_SIZE ** -0.5, 0.5)
    return dict(pair=pair, cotangent=cotangent, in_gain=in_gain, w_in=w_in, out_gain=out_gain, w_out=w_out)


EPSILON = 1e-05

def layer_norm(values, scales):
    center = values - lax.optimization_barrier(jnp.mean(values, axis=-1, keepdims=True))
    spread = lax.optimization_barrier(jnp.mean(center * center, axis=-1, keepdims=True))
    return center * lax.rsqrt(spread + EPSILON) * scales

def project_in(pair, in_gain, w_in, hidden):
    normed = layer_norm(pair.astype(jnp.float32), in_gain).astype(jnp.bfloat16)
    project = jnp.dot(normed, w_in, preferred_element_type=jnp.float32)
    left_full = jax.nn.sigmoid(project[..., :hidden]) * project[..., hidden:2 * hidden]
    right_full = jax.nn.sigmoid(project[..., 2 * hidden:3 * hidden]) * project[..., 3 * hidden:4 * hidden]
    out_gate = jax.nn.sigmoid(project[..., 4 * hidden:])
    return (normed, project, left_full, right_full, out_gate)

def project_in_grad(pair, in_gain, w_in, normed, project, left_cot, right_cot, gate_cot, hidden):
    sig_left = jax.nn.sigmoid(project[..., :hidden])
    sig_right = jax.nn.sigmoid(project[..., 2 * hidden:3 * hidden])
    sig_gate = jax.nn.sigmoid(project[..., 4 * hidden:])
    pieces = [left_cot * project[..., hidden:2 * hidden] * sig_left * (1.0 - sig_left), left_cot * sig_left, right_cot * project[..., 3 * hidden:4 * hidden] * sig_right * (1.0 - sig_right), right_cot * sig_right, gate_cot * sig_gate * (1.0 - sig_gate)]
    project_cot = jnp.concatenate(pieces, axis=-1).astype(jnp.bfloat16)
    width = normed.shape[-1]
    weight_sum = jnp.dot(normed.reshape(-1, width).T, project_cot.reshape(-1, project_cot.shape[-1]), preferred_element_type=jnp.float32)
    normed_cot = jnp.dot(project_cot, w_in.T, preferred_element_type=jnp.float32)
    unused, pullback = jax.vjp(layer_norm, pair.astype(jnp.float32), in_gain)
    pair_grad, gain_sum = pullback(normed_cot)
    return (pair_grad, gain_sum, weight_sum)

def project_out(triangle, out_gain, w_out, out_gate):
    tri_normed = layer_norm(triangle, out_gain).astype(jnp.bfloat16)
    projected = jnp.dot(tri_normed, w_out, preferred_element_type=jnp.float32)
    return (tri_normed, projected, out_gate * projected)

def project_out_grad(triangle, out_gain, w_out, out_gate, tri_normed, projected, upstream):
    gate_cot = upstream * projected
    proj_cot = (upstream * out_gate).astype(jnp.bfloat16)
    width = tri_normed.shape[-1]
    weight_sum = jnp.dot(tri_normed.reshape(-1, width).T, proj_cot.reshape(-1, proj_cot.shape[-1]), preferred_element_type=jnp.float32)
    normed_cot = jnp.dot(proj_cot, w_out.T, preferred_element_type=jnp.float32)
    unused, pullback = jax.vjp(layer_norm, triangle, out_gain)
    tri_grad, gain_sum = pullback(normed_cot)
    return (tri_grad, gain_sum, weight_sum, gate_cot)

def reference(pair, cotangent, in_gain, w_in, out_gain, w_out):
    hidden = out_gain.shape[0]
    normed, project, left_full, right_full, out_gate = project_in(pair, in_gain, w_in, hidden)
    left_act = left_full.astype(jnp.bfloat16)
    right_act = right_full.astype(jnp.bfloat16)
    triangle = jnp.einsum('ikc,jkc->ijc', left_act.astype(jnp.float32), right_act.astype(jnp.float32), precision=lax.Precision.HIGHEST)
    tri_normed, projected, update = project_out(triangle, out_gain, w_out, out_gate)
    pair_next = (pair.astype(jnp.float32) + update).astype(jnp.bfloat16)
    upstream = cotangent.astype(jnp.float32)
    tri_grad, out_gain_sum, w_out_sum, gate_cot = project_out_grad(triangle, out_gain, w_out, out_gate, tri_normed, projected, upstream)
    tri_cot = tri_grad.astype(jnp.bfloat16).astype(jnp.float32)
    left_cot = jnp.einsum('ijc,jkc->ikc', tri_cot, right_act.astype(jnp.float32), precision=lax.Precision.HIGHEST)
    right_cot = jnp.einsum('ijc,ikc->jkc', tri_cot, left_act.astype(jnp.float32), precision=lax.Precision.HIGHEST)
    pair_grad, in_gain_sum, w_in_sum = project_in_grad(pair, in_gain, w_in, normed, project, left_cot, right_cot, gate_cot, hidden)
    pair_back = (upstream + pair_grad).astype(jnp.bfloat16)
    factor = 1.0 / RES
    return (pair_next, pair_back, in_gain_sum * factor, w_in_sum * factor, out_gain_sum * factor, w_out_sum * factor)
```

```python
import itertools

import jax
import jax.numpy as jnp
from jax import lax
from jax.experimental import pallas as pl
from jax.experimental.pallas import tpu as pltpu
from jax.sharding import PartitionSpec as P

EPSILON = 1e-05
LOGICAL = pl.DeviceIdType.LOGICAL
DEVICES = 128
CHIPS = 64
CH = 128
CELLS = 2048
CHUNK = 256
TILES = CHUNK // 128
STEPS = CELLS // CHUNK
VMEM_BYTES = 63 * 2**20
F32 = jnp.float32
BF16 = jnp.bfloat16
HOPS = sorted(itertools.product((0, 1, 2), repeat=3), key=lambda hops: (-sum(hops), hops))[:-1]


def matmul(a, b):
    return jnp.dot(a, b, preferred_element_type=F32)


def matmul_nt(a, b):
    return lax.dot_general(a, b, (((1,), (1,)), ((), ())), preferred_element_type=F32)


def parts():
    row, col = lax.axis_index("row"), lax.axis_index("col")
    x, y, z, core = (row // 4) * 2 + col // 8, (col // 2) % 4, row % 4, col % 2
    xs = [((x + d) % 4 // 2) * 64 + ((x + d) % 4 % 2) * 8 for d in range(4)]
    ys = [((y + d) % 4) * 2 for d in range(4)]
    zs = [((z + d) % 4) * 16 for d in range(4)]
    return xs, ys, zs, core


def for_chips(place, act):
    for hops in HOPS:
        ways = [(1, 3) if h == 1 else (h,) for h in hops]
        for dx, dy, dz in itertools.product(*ways):
            act(place[0][dx] + place[1][dy] + place[2][dz])


def greet(place, sibling):
    barrier = pltpu.get_barrier_semaphore()

    def signal(device):
        pl.semaphore_signal(barrier, inc=1, device_id=device, device_id_type=LOGICAL)

    def act(device):
        signal(device)
        signal(device + 1)

    for_chips(place, act)
    signal(sibling)


def remote(src, dst, send, recv, device):
    return pltpu.make_async_remote_copy(
        src_ref=src, dst_ref=dst, send_sem=send, recv_sem=recv, device_id=device, device_id_type=LOGICAL
    )


def send_to(core, place, src, dst, send, recv, me):
    def act(device):
        remote(src.at[device + core], dst.at[me], send, recv, device + core).start()

    for_chips(place, act)


def send_near(sibling, src, dst, send, recv, me):
    remote(src.at[sibling], dst.at[me], send, recv, sibling).start()
    pltpu.make_async_copy(src.at[me], dst.at[me], recv).start()


def wait_all(ref, sem):
    pltpu.make_async_copy(ref, ref, sem).wait()


def wait_sent(ref, sem):
    part = ref.at[pl.ds(0, ref.shape[0] - 1)]
    pltpu.make_async_copy(part, part, sem).wait()


def block(index):
    return pl.ds(index * 128, 128)


def cells_of(chunk):
    return pl.ds(pl.multiple_of(chunk * CHUNK, CHUNK), CHUNK)


def gather_matrix(received, perm, whole):
    rows = [
        jnp.concatenate([received[:, q_hi * 4 + q_lo].reshape(128, 128) for q_lo in range(4)], axis=1)
        for q_hi in range(4)
    ]
    moved = matmul(jnp.concatenate(rows, axis=0), perm[...]).astype(BF16)
    for q_hi in range(4):
        for i_lo in range(4):
            whole[block(i_lo), block(q_hi)] = tile(moved, q_hi, i_lo)


def scatter_matrix(whole, perm, outgoing):
    whole = whole.astype(BF16)
    rows = [
        jnp.concatenate([tile(whole, i_lo, q_hi) for i_lo in range(4)], axis=1) for q_hi in range(4)
    ]
    moved = matmul(jnp.concatenate(rows, axis=0), perm[...]).astype(BF16)
    for q_hi in range(4):
        for q_lo in range(4):
            outgoing[:, q_hi * 4 + q_lo] = tile(moved, q_hi, q_lo).reshape(8, 16, 128)


def tile(value, i, j):
    return value[i * 128 : (i + 1) * 128, j * 128 : (j + 1) * 128]


def put_tiles(spread, base, chunk, value):
    for t in range(TILES):
        spread[pl.ds(base + chunk * TILES + t, 128, stride=16), :] = value[:, t * 128 : (t + 1) * 128]


def get_tiles(spread, base, chunk):
    tiles = [spread[pl.ds(base + chunk * TILES + t, 128, stride=16), :] for t in range(TILES)]
    return jnp.concatenate(tiles, axis=1)


def put_row(rows, index, value):
    rows[pl.ds(index, 128, stride=4), :] = value


def get_row(rows, index):
    return rows[pl.ds(index, 128, stride=4), :]


def sums_scatter(place, send, recv, sums, received, total, totals, first, chip, core):
    tiles = sums.reshape(CHIPS, 8, 128)

    def act(device):
        remote(
            tiles.at[device // 2], received.at[chip], send.at[first], recv.at[first], device + core
        ).start()

    for_chips(place, act)
    pltpu.make_async_copy(tiles.at[chip], received.at[chip], recv.at[first]).start()


def sums_add(sibling, send, recv, sums, received, total, totals, first, chip, core):
    wait_all(received, recv.at[first])
    total[0] = jnp.sum(received[...], axis=0) * (1.0 / 512.0)
    swap = remote(total.at[0], total.at[1], send.at[first + 1], recv.at[first + 1], sibling)
    swap.start()
    swap.wait()
    total[2] = total[0] + total[1]


def sums_gather(place, send, recv, sums, received, total, totals, first, chip, core):
    whole = totals.reshape(CHIPS, 8, 128)

    def act(device):
        remote(total.at[2], whole.at[chip], send.at[first + 2], recv.at[first + 2], device + core).start()

    for_chips(place, act)
    pltpu.make_async_copy(total.at[2], whole.at[chip], recv.at[first + 2]).start()


def kernel(
    pair_hbm,
    cot_hbm,
    in_gain_hbm,
    w_in_hbm,
    out_gain_hbm,
    w_out_hbm,
    next_hbm,
    back_hbm,
    in_gain_hbm_out,
    w_in_hbm_out,
    out_gain_hbm_out,
    w_out_hbm_out,
    next_ref,
    back_ref,
    in_gain_out,
    w_in_out,
    out_gain_out,
    w_out_out,
    pair_ref,
    cot_ref,
    in_gain_ref,
    w_in_ref,
    out_gain_ref,
    w_out_ref,
    w_in_t,
    w_out_t,
    in_gain_t,
    out_gain_t,
    perm,
    rows_perm,
    rows_perm_t,
    pair_t,
    cot_t,
    hat,
    rstd,
    normed,
    left_a,
    left_b,
    right_a,
    right_b,
    gate,
    proj_cot,
    scaled,
    tri_hat,
    tri_normed,
    spread,
    l_out,
    l_in,
    r_out,
    r_in,
    left,
    right_raw,
    right,
    tri_out,
    tri_in,
    tc_out,
    tc_in,
    tc,
    tc_t,
    lc_out,
    lc_in,
    rc_out,
    rc_in,
    project_cot,
    early_sums,
    early_in,
    early_total,
    early_totals,
    late_sums,
    late_in,
    late_total,
    late_totals,
    load,
    store,
    send,
    recv,
):
    *place, core = parts()
    me = lax.axis_index("row") * 16 + lax.axis_index("col")
    chip = me // 2
    sibling = me + 1 - 2 * core
    loads = [
        pltpu.make_async_copy(src, dst, load.at[n])
        for n, (src, dst) in enumerate(
            (
                (pair_hbm, pair_ref),
                (w_in_hbm, w_in_ref),
                (in_gain_hbm, in_gain_ref),
                (cot_hbm, cot_ref),
                (w_out_hbm, w_out_ref),
                (out_gain_hbm, out_gain_ref),
            )
        )
    ]
    for copy in loads:
        copy.start()
    greet(place, sibling)

    a = lax.broadcasted_iota(jnp.int32, (512, 512), 0)
    b = lax.broadcasted_iota(jnp.int32, (512, 512), 1)
    swapped = ((a // 32) % 4) * 128 + (a // 128) * 32 + a % 32
    perm[...] = jnp.where(swapped == b, 1.0, 0.0).astype(BF16)
    rows_perm[...] = jnp.where((a % 4) * 128 + a // 4 == b, 1.0, 0.0).astype(BF16)
    rows_perm_t[...] = jnp.where((b % 4) * 128 + b // 4 == a, 1.0, 0.0).astype(BF16)
    for copy in loads:
        copy.wait()
    for n in range(5):
        w_in_t[block(n), :] = w_in_ref[:, block(n)].T
    w_out_t[...] = w_out_ref[...].T
    in_gain_t[...] = jnp.broadcast_to(in_gain_ref[...], (128, 128)).T
    out_gain_t[...] = jnp.broadcast_to(out_gain_ref[...], (128, 128)).T

    def project(chunk, carry):
        cells = cells_of(chunk)
        x = pair_ref[cells, :].astype(F32).T
        pair_t[:, cells] = x
        center = x - jnp.mean(x, axis=0, keepdims=True)
        inverse = lax.rsqrt(jnp.mean(center * center, axis=0, keepdims=True) + EPSILON)
        x_hat = center * inverse
        hat[:, cells] = x_hat
        rstd[:, cells] = inverse
        y = (x_hat * in_gain_t[:, :1]).astype(BF16)
        normed[:, cells] = y
        for side, (keep_a, keep_b) in enumerate(((left_a, left_b), (right_a, right_b))):
            both = matmul(w_in_t[pl.ds(side * 256, 256), :], y)
            sig = jax.nn.sigmoid(both[:128])
            act = sig * both[128:]
            keep_b[:, cells] = sig
            keep_a[:, cells] = act * (1.0 - sig)
            put_tiles(spread, side * 2048, chunk, act)
        return carry

    lax.fori_loop(0, STEPS, project, 0, unroll=2)
    r_out[...] = spread[pl.ds(2048, 2048), :].astype(BF16).reshape(128, 16, 128)
    pl.semaphore_wait(pltpu.get_barrier_semaphore(), DEVICES - 1)
    right_way = (r_out, r_in, send.at[0], recv.at[0], me)
    left_way = (l_out, l_in, send.at[1], recv.at[1], me)
    send_to(0, place, *right_way)
    l_out[...] = spread[pl.ds(0, 2048), :].astype(BF16).reshape(128, 16, 128)
    send_to(0, place, *left_way)
    send_to(1, place, *right_way)
    send_near(sibling, *right_way)
    send_to(1, place, *left_way)
    send_near(sibling, *left_way)

    def upstream(chunk, carry):
        cells = cells_of(chunk)
        sig = jax.nn.sigmoid(matmul(w_in_t[pl.ds(512, 128), :], normed[:, cells]))
        gate[:, cells] = sig
        up = cot_ref[cells, :].astype(F32).T
        cot_t[:, cells] = up
        back = (up * sig).astype(BF16)
        proj_cot[:, cells] = back
        scaled[:, cells] = matmul(w_out_ref[...], back) * out_gain_t[:, :1]
        return carry

    lax.fori_loop(0, STEPS, upstream, 0)

    wait_all(r_in, recv.at[0])
    gather_matrix(r_in.reshape(8, 16, 16, 128), perm, right_raw)
    right[...] = matmul(rows_perm[...], right_raw[...]).astype(BF16)
    wait_all(l_in, recv.at[1])
    gather_matrix(l_in.reshape(8, 16, 16, 128), perm, left)
    scatter_matrix(matmul_nt(left[...], right[...]), perm, tri_out.reshape(8, 16, 16, 128))
    way = (tri_out, tri_in, send.at[2], recv.at[2], me)
    send_to(0, place, *way)
    send_to(1, place, *way)
    send_near(sibling, *way)
    wait_all(tri_in, recv.at[2])

    spread[pl.ds(0, 2048), :] = tri_in[...].reshape(2048, 128).astype(F32)

    def middle(chunk, carry):
        cells = cells_of(chunk)
        x = get_tiles(spread, 0, chunk)
        center = x - jnp.mean(x, axis=0, keepdims=True)
        inverse = lax.rsqrt(jnp.mean(center * center, axis=0, keepdims=True) + EPSILON)
        x_hat = center * inverse
        tri_hat[:, cells] = x_hat
        grad = scaled[:, cells]
        mean = jnp.mean(grad, axis=0, keepdims=True)
        along = jnp.mean(grad * x_hat, axis=0, keepdims=True)
        put_tiles(spread, 2048, chunk, inverse * (grad - mean - x_hat * along))
        return carry

    lax.fori_loop(0, STEPS, middle, 0, unroll=4)
    tc_out[...] = spread[pl.ds(2048, 2048), :].astype(BF16).reshape(128, 16, 128)
    way = (tc_out, tc_in, send.at[3], recv.at[3], me)
    send_to(0, place, *way)
    send_to(1, place, *way)
    send_near(sibling, *way)

    def update(chunk, carry):
        cells = cells_of(chunk)
        y = (tri_hat[:, cells] * out_gain_t[:, :1]).astype(BF16)
        tri_normed[:, cells] = y
        projected = matmul(w_out_t[...], y)
        sig = gate[:, cells]
        next_ref[cells, :] = (pair_t[:, cells] + sig * projected).T.astype(BF16)
        project_cot[pl.ds(512, 128), cells] = (
            cot_t[:, cells] * projected * sig * (1.0 - sig)
        ).astype(BF16)
        return carry

    lax.fori_loop(0, STEPS, update, 0)

    early = (early_sums, early_in, early_total, early_totals, 6, chip, core)
    late = (late_sums, late_in, late_total, late_totals, 9, chip, core)
    w_out_sum = matmul_nt(tri_normed[...], proj_cot[...])
    put_row(early_sums, 0, matmul_nt(normed[...], project_cot[block(4), :]))
    for n in (1, 2, 3):
        put_row(early_sums, n, w_out_sum)
    sums_scatter(place, send, recv, *early)
    next_copy = pltpu.make_async_copy(next_ref, next_hbm, store.at[0])
    next_copy.start()
    wait_all(tc_in, recv.at[3])

    gather_matrix(tc_in.reshape(8, 16, 16, 128), perm, tc)
    scatter_matrix(matmul(tc[...], right[...]), perm, lc_out.reshape(8, 16, 16, 128))
    left_way = (lc_out, lc_in, send.at[4], recv.at[4], me)
    send_to(0, place, *left_way)
    tc_t[...] = matmul_nt(rows_perm_t[...], tc[...]).astype(BF16)
    scatter_matrix(matmul(tc_t[...], left[...]), perm, rc_out.reshape(8, 16, 16, 128))
    right_way = (rc_out, rc_in, send.at[5], recv.at[5], me)
    send_to(0, place, *right_way)
    send_to(1, place, *left_way)
    send_near(sibling, *left_way)
    send_to(1, place, *right_way)
    send_near(sibling, *right_way)

    sums_add(sibling, send, recv, *early)

    for side, (got, keep_a, keep_b) in enumerate(((lc_in, left_a, left_b), (rc_in, right_a, right_b))):
        wait_all(got, recv.at[4 + side])
        spread[pl.ds(side * 2048, 2048), :] = got[...].reshape(2048, 128).astype(F32)

        def products(chunk, carry):
            cells = cells_of(chunk)
            grad = get_tiles(spread, side * 2048, chunk)
            project_cot[pl.ds(side * 256, 128), cells] = (grad * keep_a[:, cells]).astype(BF16)
            project_cot[pl.ds(side * 256 + 128, 128), cells] = (grad * keep_b[:, cells]).astype(BF16)
            return carry

        lax.fori_loop(0, STEPS, products, 0, unroll=4)
        part = matmul_nt(normed[...], project_cot[pl.ds(side * 256, 256), :])
        put_row(late_sums, 2 * side, part[:, :128])
        put_row(late_sums, 2 * side + 1, part[:, 128:])

    sums_scatter(place, send, recv, *late)
    sums_gather(place, send, recv, *early)

    def finish(chunk, carry):
        cells = cells_of(chunk)
        grad = matmul(w_in_ref[...], project_cot[:, cells]) * in_gain_t[:, :1]
        x_hat = hat[:, cells]
        mean = jnp.mean(grad, axis=0, keepdims=True)
        along = jnp.mean(grad * x_hat, axis=0, keepdims=True)
        back = rstd[:, cells] * (grad - mean - x_hat * along)
        back_ref[cells, :] = (cot_t[:, cells] + back).T.astype(BF16)
        return carry

    lax.fori_loop(0, STEPS, finish, 0, unroll=2)
    back_copy = pltpu.make_async_copy(back_ref, back_hbm, store.at[1])
    back_copy.start()
    sums_add(sibling, send, recv, *late)
    sums_gather(place, send, recv, *late)
    wait_all(early_totals, recv.at[8])
    wait_all(late_totals, recv.at[11])

    along = jnp.zeros((128, 128), F32)
    for n in range(5):
        part = get_row(early_totals, 0) if n == 4 else get_row(late_totals, n)
        w_in_out[:, block(n)] = part
        along += part * w_in_ref[:, block(n)].astype(F32)
    in_gain_out[...] = jnp.sum((along / in_gain_t[...]).T, axis=0, keepdims=True)
    part = get_row(early_totals, 1)
    w_out_out[...] = part
    along = part * w_out_ref[...].astype(F32) / out_gain_t[...]
    out_gain_out[...] = jnp.sum(along.T, axis=0, keepdims=True)

    stores = [next_copy, back_copy] + [
        pltpu.make_async_copy(src, dst, store.at[2 + n])
        for n, (src, dst) in enumerate(
            (
                (in_gain_out, in_gain_hbm_out),
                (w_in_out, w_in_hbm_out),
                (out_gain_out, out_gain_hbm_out),
                (w_out_out, w_out_hbm_out),
            )
        )
    ]
    for copy in stores[2:]:
        copy.start()
    for copy in stores:
        copy.wait()
    wait_sent(r_out, send.at[0])
    wait_sent(l_out, send.at[1])
    wait_sent(tri_out, send.at[2])
    wait_sent(tc_out, send.at[3])
    wait_sent(lc_out, send.at[4])
    wait_sent(rc_out, send.at[5])
    for n in (6, 8, 9, 11):
        wait_sent(early_in, send.at[n])


def deliver(*refs):
    srcs, dsts, holds = refs[:6], refs[6:12], refs[12:18]
    load, store = refs[18:]
    loads = [pltpu.make_async_copy(src, hold, load.at[n]) for n, (src, hold) in enumerate(zip(srcs, holds))]
    stores = [pltpu.make_async_copy(hold, dst, store.at[n]) for n, (hold, dst) in enumerate(zip(holds, dsts))]
    for copy in loads:
        copy.start()
    for first, second in zip(loads, stores):
        first.wait()
        second.start()
    for copy in stores:
        copy.wait()


def on_device(pair, cotangent, in_gain, w_in, out_gain, w_out):
    hbm = pl.BlockSpec(memory_space=pltpu.HBM)

    def bf(*shape):
        return pltpu.VMEM(shape, BF16)

    def fl(*shape):
        return pltpu.VMEM(shape, F32)

    scratch = [
        bf(2048, 128),
        bf(2048, 128),
        fl(1, 128),
        fl(128, 640),
        fl(1, 128),
        fl(128, 128),
        bf(2048, 128),
        bf(2048, 128),
        fl(1, 128),
        bf(128, 640),
        fl(1, 128),
        bf(128, 128),
        bf(640, 128),
        bf(128, 128),
        fl(128, 128),
        fl(128, 128),
        bf(512, 512),
        bf(512, 512),
        bf(512, 512),
        fl(128, 2048),
        fl(128, 2048),
        fl(128, 2048),
        fl(1, 2048),
        bf(128, 2048),
        fl(128, 2048),
        fl(128, 2048),
        fl(128, 2048),
        fl(128, 2048),
        fl(128, 2048),
        bf(128, 2048),
        fl(128, 2048),
        fl(128, 2048),
        bf(128, 2048),
        fl(4096, 128),
        bf(128, 16, 128),
        bf(128, 16, 128),
        bf(128, 16, 128),
        bf(128, 16, 128),
        bf(512, 512),
        bf(512, 512),
        bf(512, 512),
        bf(128, 16, 128),
        bf(128, 16, 128),
        bf(128, 16, 128),
        bf(128, 16, 128),
        bf(512, 512),
        bf(512, 512),
        bf(128, 16, 128),
        bf(128, 16, 128),
        bf(128, 16, 128),
        bf(128, 16, 128),
        bf(640, 2048),
        fl(512, 128),
        fl(64, 8, 128),
        fl(3, 8, 128),
        fl(512, 128),
        fl(512, 128),
        fl(64, 8, 128),
        fl(3, 8, 128),
        fl(512, 128),
        pltpu.SemaphoreType.DMA((6,)),
        pltpu.SemaphoreType.DMA((6,)),
        pltpu.SemaphoreType.DMA((12,)),
        pltpu.SemaphoreType.DMA((12,)),
    ]
    shapes = [
        jax.ShapeDtypeStruct((CELLS, CH), BF16),
        jax.ShapeDtypeStruct((CELLS, CH), BF16),
        jax.ShapeDtypeStruct((1, CH), F32),
        jax.ShapeDtypeStruct((CH, 640), F32),
        jax.ShapeDtypeStruct((1, CH), F32),
        jax.ShapeDtypeStruct((CH, CH), F32),
    ]
    results = pl.pallas_call(
        kernel,
        out_shape=shapes,
        in_specs=[hbm] * 6,
        out_specs=[hbm] * 6,
        scratch_shapes=scratch,
        compiler_params=pltpu.CompilerParams(
            collective_id=0, has_side_effects=True, vmem_limit_bytes=VMEM_BYTES
        ),
        name="triangle_update",
    )(
        pair.reshape(CELLS, CH),
        cotangent.reshape(CELLS, CH),
        in_gain.reshape(1, CH),
        w_in,
        out_gain.reshape(1, CH),
        w_out,
    )
    pair_next, pair_back, in_gain_grad, w_in_grad, out_gain_grad, w_out_grad = pl.pallas_call(
        deliver,
        out_shape=shapes,
        in_specs=[hbm] * 6,
        out_specs=[hbm] * 6,
        scratch_shapes=[
            *(pltpu.VMEM(shape.shape, shape.dtype) for shape in shapes),
            pltpu.SemaphoreType.DMA((6,)),
            pltpu.SemaphoreType.DMA((6,)),
        ],
        compiler_params=pltpu.CompilerParams(vmem_limit_bytes=VMEM_BYTES),
        name="deliver",
    )(*results)
    return (
        pair_next.reshape(64, 32, CH),
        pair_back.reshape(64, 32, CH),
        in_gain_grad.reshape(CH),
        w_in_grad,
        out_gain_grad.reshape(CH),
        w_out_grad,
    )


def solution(mesh):
    in_specs = (P("row", "col", None), P("row", "col", None), P(), P(), P(), P())
    out_specs = (P("row", "col", None), P("row", "col", None), P(), P(), P(), P())
    return jax.shard_map(
        on_device, mesh=mesh, in_specs=in_specs, out_specs=out_specs, check_vma=False
    )
```

```python
import itertools

import jax
import jax.numpy as jnp
from jax import lax
from jax.experimental import pallas as pl
from jax.experimental.pallas import tpu as pltpu
from jax.sharding import PartitionSpec as P

EPSILON = 1e-05
LOGICAL = pl.DeviceIdType.LOGICAL
DEVICES = 128
CHIPS = 64
CH = 128
CELLS = 2048
CHUNK = 256
TILES = CHUNK // 128
STEPS = CELLS // CHUNK
VMEM_BYTES = 63 * 2**20
F32 = jnp.float32
BF16 = jnp.bfloat16
HOPS = sorted(itertools.product((0, 1, 2), repeat=3), key=lambda hops: (-sum(hops), hops))[:-1]


def matmul(a, b):
    return jnp.dot(a, b, preferred_element_type=F32)


def matmul_nt(a, b):
    return lax.dot_general(a, b, (((1,), (1,)), ((), ())), preferred_element_type=F32)


def parts():
    row, col = lax.axis_index("row"), lax.axis_index("col")
    x, y, z, core = (row // 4) * 2 + col // 8, (col // 2) % 4, row % 4, col % 2
    xs = [((x + d) % 4 // 2) * 64 + ((x + d) % 4 % 2) * 8 for d in range(4)]
    ys = [((y + d) % 4) * 2 for d in range(4)]
    zs = [((z + d) % 4) * 16 for d in range(4)]
    return xs, ys, zs, core


def for_chips(place, act):
    for hops in HOPS:
        ways = [(1, 3) if h == 1 else (h,) for h in hops]
        for dx, dy, dz in itertools.product(*ways):
            act(place[0][dx] + place[1][dy] + place[2][dz])


def greet(place, sibling):
    barrier = pltpu.get_barrier_semaphore()

    def signal(device):
        pl.semaphore_signal(barrier, inc=1, device_id=device, device_id_type=LOGICAL)

    def act(device):
        signal(device)
        signal(device + 1)

    for_chips(place, act)
    signal(sibling)


def remote(src, dst, send, recv, device):
    return pltpu.make_async_remote_copy(
        src_ref=src, dst_ref=dst, send_sem=send, recv_sem=recv, device_id=device, device_id_type=LOGICAL
    )


def send_to(core, place, src, dst, send, recv, me):
    def act(device):
        remote(src.at[device + core], dst.at[me], send, recv, device + core).start()

    for_chips(place, act)


def send_near(sibling, src, dst, send, recv, me):
    remote(src.at[sibling], dst.at[me], send, recv, sibling).start()
    pltpu.make_async_copy(src.at[me], dst.at[me], recv).start()


def wait_all(ref, sem):
    pltpu.make_async_copy(ref, ref, sem).wait()


def wait_sent(ref, sem):
    part = ref.at[pl.ds(0, ref.shape[0] - 1)]
    pltpu.make_async_copy(part, part, sem).wait()


def block(index):
    return pl.ds(index * 128, 128)


def cells_of(chunk):
    return pl.ds(pl.multiple_of(chunk * CHUNK, CHUNK), CHUNK)


def gather_matrix(received, perm, whole):
    rows = [
        jnp.concatenate([received[:, q_hi * 4 + q_lo].reshape(128, 128) for q_lo in range(4)], axis=1)
        for q_hi in range(4)
    ]
    moved = matmul(jnp.concatenate(rows, axis=0), perm[...]).astype(BF16)
    for q_hi in range(4):
        for i_lo in range(4):
            whole[block(i_lo), block(q_hi)] = tile(moved, q_hi, i_lo)


def scatter_matrix(whole, perm, outgoing):
    whole = whole.astype(BF16)
    rows = [
        jnp.concatenate([tile(whole, i_lo, q_hi) for i_lo in range(4)], axis=1) for q_hi in range(4)
    ]
    moved = matmul(jnp.concatenate(rows, axis=0), perm[...]).astype(BF16)
    for q_hi in range(4):
        for q_lo in range(4):
            outgoing[:, q_hi * 4 + q_lo] = tile(moved, q_hi, q_lo).reshape(8, 16, 128)


def tile(value, i, j):
    return value[i * 128 : (i + 1) * 128, j * 128 : (j + 1) * 128]


def put_tiles(spread, base, chunk, value):
    for t in range(TILES):
        spread[pl.ds(base + chunk * TILES + t, 128, stride=16), :] = value[:, t * 128 : (t + 1) * 128]


def get_tiles(spread, base, chunk):
    tiles = [spread[pl.ds(base + chunk * TILES + t, 128, stride=16), :] for t in range(TILES)]
    return jnp.concatenate(tiles, axis=1)


def put_row(rows, index, value):
    rows[pl.ds(index, 128, stride=4), :] = value


def get_row(rows, index):
    return rows[pl.ds(index, 128, stride=4), :]


def sums_scatter(place, send, recv, sums, received, total, totals, first, chip, core):
    tiles = sums.reshape(CHIPS, 8, 128)

    def act(device):
        remote(
            tiles.at[device // 2], received.at[chip], send.at[first], recv.at[first], device + core
        ).start()

    for_chips(place, act)
    pltpu.make_async_copy(tiles.at[chip], received.at[chip], recv.at[first]).start()


def sums_add(sibling, send, recv, sums, received, total, totals, first, chip, core):
    wait_all(received, recv.at[first])
    total[0] = jnp.sum(received[...], axis=0) * (1.0 / 512.0)
    swap = remote(total.at[0], total.at[1], send.at[first + 1], recv.at[first + 1], sibling)
    swap.start()
    swap.wait()
    total[2] = total[0] + total[1]


def sums_gather(place, send, recv, sums, received, total, totals, first, chip, core):
    whole = totals.reshape(CHIPS, 8, 128)

    def act(device):
        remote(total.at[2], whole.at[chip], send.at[first + 2], recv.at[first + 2], device + core).start()

    for_chips(place, act)
    pltpu.make_async_copy(total.at[2], whole.at[chip], recv.at[first + 2]).start()


def kernel(
    pair_hbm,
    cot_hbm,
    in_gain_hbm,
    w_in_hbm,
    out_gain_hbm,
    w_out_hbm,
    next_hbm,
    back_hbm,
    early_totals,
    late_totals,
    next_ref,
    back_ref,
    pair_ref,
    cot_ref,
    in_gain_ref,
    w_in_ref,
    out_gain_ref,
    w_out_ref,
    w_in_t,
    w_out_t,
    in_gain_t,
    out_gain_t,
    perm,
    rows_perm,
    rows_perm_t,
    pair_t,
    cot_t,
    hat,
    rstd,
    normed,
    left_a,
    left_b,
    right_a,
    right_b,
    gate,
    proj_cot,
    scaled,
    tri_hat,
    tri_normed,
    spread,
    l_out,
    l_in,
    r_out,
    r_in,
    left,
    right_raw,
    right,
    tri_out,
    tri_in,
    tc_out,
    tc_in,
    tc,
    tc_t,
    lc_out,
    lc_in,
    rc_out,
    rc_in,
    project_cot,
    early_sums,
    early_in,
    early_total,
    late_sums,
    late_in,
    late_total,
    load,
    store,
    send,
    recv,
):
    *place, core = parts()
    me = lax.axis_index("row") * 16 + lax.axis_index("col")
    chip = me // 2
    sibling = me + 1 - 2 * core
    loads = [
        pltpu.make_async_copy(src, dst, load.at[n])
        for n, (src, dst) in enumerate(
            (
                (pair_hbm, pair_ref),
                (w_in_hbm, w_in_ref),
                (in_gain_hbm, in_gain_ref),
                (cot_hbm, cot_ref),
                (w_out_hbm, w_out_ref),
                (out_gain_hbm, out_gain_ref),
            )
        )
    ]
    for copy in loads:
        copy.start()
    greet(place, sibling)

    a = lax.broadcasted_iota(jnp.int32, (512, 512), 0)
    b = lax.broadcasted_iota(jnp.int32, (512, 512), 1)
    swapped = ((a // 32) % 4) * 128 + (a // 128) * 32 + a % 32
    perm[...] = jnp.where(swapped == b, 1.0, 0.0).astype(BF16)
    rows_perm[...] = jnp.where((a % 4) * 128 + a // 4 == b, 1.0, 0.0).astype(BF16)
    rows_perm_t[...] = jnp.where((b % 4) * 128 + b // 4 == a, 1.0, 0.0).astype(BF16)
    for copy in loads:
        copy.wait()
    for n in range(5):
        w_in_t[block(n), :] = w_in_ref[:, block(n)].T
    w_out_t[...] = w_out_ref[...].T
    in_gain_t[...] = jnp.broadcast_to(in_gain_ref[...], (128, 128)).T
    out_gain_t[...] = jnp.broadcast_to(out_gain_ref[...], (128, 128)).T

    def project(chunk, carry):
        cells = cells_of(chunk)
        x = pair_ref[cells, :].astype(F32).T
        pair_t[:, cells] = x
        center = x - jnp.mean(x, axis=0, keepdims=True)
        inverse = lax.rsqrt(jnp.mean(center * center, axis=0, keepdims=True) + EPSILON)
        x_hat = center * inverse
        hat[:, cells] = x_hat
        rstd[:, cells] = inverse
        y = (x_hat * in_gain_t[:, :1]).astype(BF16)
        normed[:, cells] = y
        for side, (keep_a, keep_b) in enumerate(((left_a, left_b), (right_a, right_b))):
            both = matmul(w_in_t[pl.ds(side * 256, 256), :], y)
            sig = jax.nn.sigmoid(both[:128])
            act = sig * both[128:]
            keep_b[:, cells] = sig
            keep_a[:, cells] = act * (1.0 - sig)
            put_tiles(spread, side * 2048, chunk, act)
        return carry

    lax.fori_loop(0, STEPS, project, 0, unroll=4)
    r_out[...] = spread[pl.ds(2048, 2048), :].astype(BF16).reshape(128, 16, 128)
    pl.semaphore_wait(pltpu.get_barrier_semaphore(), DEVICES - 1)
    right_way = (r_out, r_in, send.at[0], recv.at[0], me)
    left_way = (l_out, l_in, send.at[1], recv.at[1], me)
    send_to(0, place, *right_way)
    l_out[...] = spread[pl.ds(0, 2048), :].astype(BF16).reshape(128, 16, 128)
    send_to(0, place, *left_way)
    send_to(1, place, *right_way)
    send_near(sibling, *right_way)
    send_to(1, place, *left_way)
    send_near(sibling, *left_way)

    def upstream(chunk, carry):
        cells = cells_of(chunk)
        sig = jax.nn.sigmoid(matmul(w_in_t[pl.ds(512, 128), :], normed[:, cells]))
        gate[:, cells] = sig
        up = cot_ref[cells, :].astype(F32).T
        cot_t[:, cells] = up
        back = (up * sig).astype(BF16)
        proj_cot[:, cells] = back
        scaled[:, cells] = matmul(w_out_ref[...], back) * out_gain_t[:, :1]
        return carry

    lax.fori_loop(0, STEPS, upstream, 0)

    wait_all(r_in, recv.at[0])
    gather_matrix(r_in.reshape(8, 16, 16, 128), perm, right_raw)
    right[...] = matmul(rows_perm[...], right_raw[...]).astype(BF16)
    wait_all(l_in, recv.at[1])
    gather_matrix(l_in.reshape(8, 16, 16, 128), perm, left)
    scatter_matrix(matmul_nt(left[...], right[...]), perm, tri_out.reshape(8, 16, 16, 128))
    way = (tri_out, tri_in, send.at[2], recv.at[2], me)
    send_to(0, place, *way)
    send_to(1, place, *way)
    send_near(sibling, *way)
    wait_all(tri_in, recv.at[2])

    spread[pl.ds(0, 2048), :] = tri_in[...].reshape(2048, 128).astype(F32)

    def middle(chunk, carry):
        cells = cells_of(chunk)
        x = get_tiles(spread, 0, chunk)
        center = x - jnp.mean(x, axis=0, keepdims=True)
        inverse = lax.rsqrt(jnp.mean(center * center, axis=0, keepdims=True) + EPSILON)
        x_hat = center * inverse
        tri_hat[:, cells] = x_hat
        grad = scaled[:, cells]
        mean = jnp.mean(grad, axis=0, keepdims=True)
        along = jnp.mean(grad * x_hat, axis=0, keepdims=True)
        put_tiles(spread, 2048, chunk, inverse * (grad - mean - x_hat * along))
        return carry

    lax.fori_loop(0, STEPS, middle, 0, unroll=True)
    tc_out[...] = spread[pl.ds(2048, 2048), :].astype(BF16).reshape(128, 16, 128)
    way = (tc_out, tc_in, send.at[3], recv.at[3], me)
    send_to(0, place, *way)
    send_to(1, place, *way)
    send_near(sibling, *way)

    def update(chunk, carry):
        cells = cells_of(chunk)
        y = (tri_hat[:, cells] * out_gain_t[:, :1]).astype(BF16)
        tri_normed[:, cells] = y
        projected = matmul(w_out_t[...], y)
        sig = gate[:, cells]
        next_ref[cells, :] = (pair_t[:, cells] + sig * projected).T.astype(BF16)
        project_cot[pl.ds(512, 128), cells] = (
            cot_t[:, cells] * projected * sig * (1.0 - sig)
        ).astype(BF16)
        return carry

    lax.fori_loop(0, STEPS, update, 0)

    early = (early_sums, early_in, early_total, early_totals, 6, chip, core)
    late = (late_sums, late_in, late_total, late_totals, 9, chip, core)
    w_out_sum = matmul_nt(tri_normed[...], proj_cot[...])
    put_row(early_sums, 0, matmul_nt(normed[...], project_cot[block(4), :]))
    for n in (1, 2, 3):
        put_row(early_sums, n, w_out_sum)
    sums_scatter(place, send, recv, *early)
    next_copy = pltpu.make_async_copy(next_ref, next_hbm, store.at[0])
    next_copy.start()
    wait_all(tc_in, recv.at[3])

    gather_matrix(tc_in.reshape(8, 16, 16, 128), perm, tc)
    scatter_matrix(matmul(tc[...], right[...]), perm, lc_out.reshape(8, 16, 16, 128))
    left_way = (lc_out, lc_in, send.at[4], recv.at[4], me)
    send_to(0, place, *left_way)
    tc_t[...] = matmul_nt(rows_perm_t[...], tc[...]).astype(BF16)
    scatter_matrix(matmul(tc_t[...], left[...]), perm, rc_out.reshape(8, 16, 16, 128))
    right_way = (rc_out, rc_in, send.at[5], recv.at[5], me)
    send_to(0, place, *right_way)
    send_to(1, place, *left_way)
    send_near(sibling, *left_way)
    send_to(1, place, *right_way)
    send_near(sibling, *right_way)

    sums_add(sibling, send, recv, *early)

    for side, (got, keep_a, keep_b) in enumerate(((lc_in, left_a, left_b), (rc_in, right_a, right_b))):
        wait_all(got, recv.at[4 + side])
        spread[pl.ds(side * 2048, 2048), :] = got[...].reshape(2048, 128).astype(F32)

        def products(chunk, carry):
            cells = cells_of(chunk)
            grad = get_tiles(spread, side * 2048, chunk)
            project_cot[pl.ds(side * 256, 128), cells] = (grad * keep_a[:, cells]).astype(BF16)
            project_cot[pl.ds(side * 256 + 128, 128), cells] = (grad * keep_b[:, cells]).astype(BF16)
            return carry

        lax.fori_loop(0, STEPS, products, 0, unroll=True)
        part = matmul_nt(normed[...], project_cot[pl.ds(side * 256, 256), :])
        put_row(late_sums, 2 * side, part[:, :128])
        put_row(late_sums, 2 * side + 1, part[:, 128:])

    sums_scatter(place, send, recv, *late)
    sums_gather(place, send, recv, *early)

    def finish(chunk, carry):
        cells = cells_of(chunk)
        grad = matmul(w_in_ref[...], project_cot[:, cells]) * in_gain_t[:, :1]
        x_hat = hat[:, cells]
        mean = jnp.mean(grad, axis=0, keepdims=True)
        along = jnp.mean(grad * x_hat, axis=0, keepdims=True)
        back = rstd[:, cells] * (grad - mean - x_hat * along)
        back_ref[cells, :] = (cot_t[:, cells] + back).T.astype(BF16)
        return carry

    lax.fori_loop(0, STEPS, finish, 0, unroll=2)
    back_copy = pltpu.make_async_copy(back_ref, back_hbm, store.at[1])
    back_copy.start()
    sums_add(sibling, send, recv, *late)
    sums_gather(place, send, recv, *late)
    wait_all(early_totals, recv.at[8])
    wait_all(late_totals, recv.at[11])

    next_copy.wait()
    back_copy.wait()
    wait_sent(r_out, send.at[0])
    wait_sent(l_out, send.at[1])
    wait_sent(tri_out, send.at[2])
    wait_sent(tc_out, send.at[3])
    wait_sent(lc_out, send.at[4])
    wait_sent(rc_out, send.at[5])
    for n in (6, 8, 9, 11):
        wait_sent(early_in, send.at[n])


def deliver(
    next_hbm,
    back_hbm,
    early_hbm,
    late_hbm,
    in_gain_hbm,
    w_in_hbm,
    out_gain_hbm,
    w_out_hbm,
    next_out,
    back_out,
    in_gain_grad_out,
    w_in_grad_out,
    out_gain_grad_out,
    w_out_grad_out,
    next_ref,
    back_ref,
    early,
    late,
    in_gain,
    w_in,
    out_gain,
    w_out,
    in_gain_grad,
    w_in_grad,
    out_gain_grad,
    w_out_grad,
    load,
    store,
):
    sources = (early_hbm, late_hbm, in_gain_hbm, w_in_hbm, out_gain_hbm, w_out_hbm, next_hbm, back_hbm)
    holds = (early, late, in_gain, w_in, out_gain, w_out, next_ref, back_ref)
    loads = [pltpu.make_async_copy(src, dst, load.at[n]) for n, (src, dst) in enumerate(zip(sources, holds))]
    results = (next_ref, back_ref, in_gain_grad, w_in_grad, out_gain_grad, w_out_grad)
    places = (next_out, back_out, in_gain_grad_out, w_in_grad_out, out_gain_grad_out, w_out_grad_out)
    stores = [pltpu.make_async_copy(src, dst, store.at[n]) for n, (src, dst) in enumerate(zip(results, places))]
    for copy in loads:
        copy.start()
    for n in (0, 1):
        loads[6 + n].wait()
        stores[n].start()
    for copy in loads[:6]:
        copy.wait()
    along = jnp.zeros((128, 128), F32)
    for n in range(5):
        part = get_row(early, 0) if n == 4 else get_row(late, n)
        w_in_grad[:, block(n)] = part
        along += part * w_in[:, block(n)].astype(F32)
    stores[3].start()
    part = get_row(early, 1)
    w_out_grad[...] = part
    stores[5].start()
    in_gain_grad[...] = jnp.sum(along.T, axis=0, keepdims=True) / in_gain[...]
    along = part * w_out[...].astype(F32)
    out_gain_grad[...] = jnp.sum(along.T, axis=0, keepdims=True) / out_gain[...]
    stores[2].start()
    stores[4].start()
    for copy in stores:
        copy.wait()


def on_device(pair, cotangent, in_gain, w_in, out_gain, w_out):
    hbm = pl.BlockSpec(memory_space=pltpu.HBM)

    def bf(*shape):
        return pltpu.VMEM(shape, BF16)

    def fl(*shape):
        return pltpu.VMEM(shape, F32)

    scratch = [
        bf(2048, 128),
        bf(2048, 128),
        bf(2048, 128),
        bf(2048, 128),
        fl(1, 128),
        bf(128, 640),
        fl(1, 128),
        bf(128, 128),
        bf(640, 128),
        bf(128, 128),
        fl(128, 128),
        fl(128, 128),
        bf(512, 512),
        bf(512, 512),
        bf(512, 512),
        fl(128, 2048),
        fl(128, 2048),
        fl(128, 2048),
        fl(1, 2048),
        bf(128, 2048),
        fl(128, 2048),
        fl(128, 2048),
        fl(128, 2048),
        fl(128, 2048),
        fl(128, 2048),
        bf(128, 2048),
        fl(128, 2048),
        fl(128, 2048),
        bf(128, 2048),
        fl(4096, 128),
        bf(128, 16, 128),
        bf(128, 16, 128),
        bf(128, 16, 128),
        bf(128, 16, 128),
        bf(512, 512),
        bf(512, 512),
        bf(512, 512),
        bf(128, 16, 128),
        bf(128, 16, 128),
        bf(128, 16, 128),
        bf(128, 16, 128),
        bf(512, 512),
        bf(512, 512),
        bf(128, 16, 128),
        bf(128, 16, 128),
        bf(128, 16, 128),
        bf(128, 16, 128),
        bf(640, 2048),
        fl(512, 128),
        fl(64, 8, 128),
        fl(3, 8, 128),
        fl(512, 128),
        fl(64, 8, 128),
        fl(3, 8, 128),
        pltpu.SemaphoreType.DMA((6,)),
        pltpu.SemaphoreType.DMA((2,)),
        pltpu.SemaphoreType.DMA((12,)),
        pltpu.SemaphoreType.DMA((12,)),
    ]
    shapes = [
        jax.ShapeDtypeStruct((CELLS, CH), BF16),
        jax.ShapeDtypeStruct((CELLS, CH), BF16),
        jax.ShapeDtypeStruct((1, CH), F32),
        jax.ShapeDtypeStruct((CH, 640), F32),
        jax.ShapeDtypeStruct((1, CH), F32),
        jax.ShapeDtypeStruct((CH, CH), F32),
    ]
    params = (in_gain.reshape(1, CH), w_in, out_gain.reshape(1, CH), w_out)
    sums_shape = jax.ShapeDtypeStruct((512, 128), F32)
    results = pl.pallas_call(
        kernel,
        out_shape=shapes[:2] + [sums_shape] * 2,
        in_specs=[hbm] * 6,
        out_specs=[hbm] * 4,
        scratch_shapes=scratch,
        compiler_params=pltpu.CompilerParams(
            collective_id=0, has_side_effects=True, vmem_limit_bytes=VMEM_BYTES
        ),
        name="triangle_update",
    )(pair.reshape(CELLS, CH), cotangent.reshape(CELLS, CH), *params)
    pair_next, pair_back, in_gain_grad, w_in_grad, out_gain_grad, w_out_grad = pl.pallas_call(
        deliver,
        out_shape=shapes,
        in_specs=[hbm] * 8,
        out_specs=[hbm] * 6,
        scratch_shapes=[
            bf(CELLS, CH),
            bf(CELLS, CH),
            fl(512, 128),
            fl(512, 128),
            fl(1, CH),
            bf(CH, 640),
            fl(1, CH),
            bf(CH, CH),
            fl(1, CH),
            fl(CH, 640),
            fl(1, CH),
            fl(CH, CH),
            pltpu.SemaphoreType.DMA((8,)),
            pltpu.SemaphoreType.DMA((6,)),
        ],
        compiler_params=pltpu.CompilerParams(vmem_limit_bytes=VMEM_BYTES),
        name="deliver",
    )(*results, *params)
    return (
        pair_next.reshape(64, 32, CH),
        pair_back.reshape(64, 32, CH),
        in_gain_grad.reshape(CH),
        w_in_grad,
        out_gain_grad.reshape(CH),
        w_out_grad,
    )


def solution(mesh):
    in_specs = (P("row", "col", None), P("row", "col", None), P(), P(), P(), P())
    out_specs = (P("row", "col", None), P("row", "col", None), P(), P(), P(), P())
    return jax.shard_map(
        on_device, mesh=mesh, in_specs=in_specs, out_specs=out_specs, check_vma=False
    )
```

```python
import itertools

import jax
import jax.numpy as jnp
from jax import lax
from jax.experimental import pallas as pl
from jax.experimental.pallas import tpu as pltpu
from jax.sharding import PartitionSpec as P

EPSILON = 1e-05
LOGICAL = pl.DeviceIdType.LOGICAL
DEVICES = 128
CHIPS = 64
CH = 128
CELLS = 2048
CHUNK = 256
TILES = CHUNK // 128
STEPS = CELLS // CHUNK
VMEM_BYTES = 63 * 2**20
F32 = jnp.float32
BF16 = jnp.bfloat16
HOPS = sorted(itertools.product((0, 1, 2), repeat=3), key=lambda hops: (-sum(hops), hops))[:-1]


def matmul(a, b):
    return jnp.dot(a, b, preferred_element_type=F32)


def matmul_nt(a, b):
    return lax.dot_general(a, b, (((1,), (1,)), ((), ())), preferred_element_type=F32)


def parts():
    row, col = lax.axis_index("row"), lax.axis_index("col")
    x, y, z, core = (row // 4) * 2 + col // 8, (col // 2) % 4, row % 4, col % 2
    xs = [((x + d) % 4 // 2) * 64 + ((x + d) % 4 % 2) * 8 for d in range(4)]
    ys = [((y + d) % 4) * 2 for d in range(4)]
    zs = [((z + d) % 4) * 16 for d in range(4)]
    return xs, ys, zs, core


def for_chips(place, act):
    for hops in HOPS:
        ways = [(1, 3) if h == 1 else (h,) for h in hops]
        for dx, dy, dz in itertools.product(*ways):
            act(place[0][dx] + place[1][dy] + place[2][dz])


def greet(place, sibling):
    barrier = pltpu.get_barrier_semaphore()

    def signal(device):
        pl.semaphore_signal(barrier, inc=1, device_id=device, device_id_type=LOGICAL)

    def act(device):
        signal(device)
        signal(device + 1)

    for_chips(place, act)
    signal(sibling)


def remote(src, dst, send, recv, device):
    return pltpu.make_async_remote_copy(
        src_ref=src, dst_ref=dst, send_sem=send, recv_sem=recv, device_id=device, device_id_type=LOGICAL
    )


def send_to(core, place, src, dst, send, recv, me):
    def act(device):
        remote(src.at[device + core], dst.at[me], send, recv, device + core).start()

    for_chips(place, act)


def send_near(sibling, src, dst, send, recv, me):
    remote(src.at[sibling], dst.at[me], send, recv, sibling).start()
    pltpu.make_async_copy(src.at[me], dst.at[me], recv).start()


def wait_all(ref, sem):
    pltpu.make_async_copy(ref, ref, sem).wait()


def wait_sent(ref, sem):
    part = ref.at[pl.ds(0, ref.shape[0] - 1)]
    pltpu.make_async_copy(part, part, sem).wait()


def block(index):
    return pl.ds(index * 128, 128)


def cells_of(chunk):
    return pl.ds(pl.multiple_of(chunk * CHUNK, CHUNK), CHUNK)


def gather_matrix(received, perm, whole):
    rows = [
        jnp.concatenate([received[:, q_hi * 4 + q_lo].reshape(128, 128) for q_lo in range(4)], axis=1)
        for q_hi in range(4)
    ]
    moved = matmul(jnp.concatenate(rows, axis=0), perm[...]).astype(BF16)
    for q_hi in range(4):
        for i_lo in range(4):
            whole[block(i_lo), block(q_hi)] = tile(moved, q_hi, i_lo)


def scatter_matrix(whole, perm, outgoing):
    whole = whole.astype(BF16)
    rows = [
        jnp.concatenate([tile(whole, i_lo, q_hi) for i_lo in range(4)], axis=1) for q_hi in range(4)
    ]
    moved = matmul(jnp.concatenate(rows, axis=0), perm[...]).astype(BF16)
    for q_hi in range(4):
        for q_lo in range(4):
            outgoing[:, q_hi * 4 + q_lo] = tile(moved, q_hi, q_lo).reshape(8, 16, 128)


def tile(value, i, j):
    return value[i * 128 : (i + 1) * 128, j * 128 : (j + 1) * 128]


def put_tiles(spread, base, chunk, value):
    for t in range(TILES):
        spread[pl.ds(base + chunk * TILES + t, 128, stride=16), :] = value[:, t * 128 : (t + 1) * 128]


def get_tiles(spread, base, chunk):
    tiles = [spread[pl.ds(base + chunk * TILES + t, 128, stride=16), :] for t in range(TILES)]
    return jnp.concatenate(tiles, axis=1)


def put_row(rows, index, value):
    rows[pl.ds(index, 128, stride=4), :] = value


def get_row(rows, index):
    return rows[pl.ds(index, 128, stride=4), :]


def sums_scatter(place, send, recv, sums, received, total, totals, first, chip, core):
    tiles = sums.reshape(CHIPS, 8, 128)

    def act(device):
        remote(
            tiles.at[device // 2], received.at[chip], send.at[first], recv.at[first], device + core
        ).start()

    for_chips(place, act)
    pltpu.make_async_copy(tiles.at[chip], received.at[chip], recv.at[first]).start()


def sums_add(sibling, send, recv, sums, received, total, totals, first, chip, core):
    wait_all(received, recv.at[first])
    total[0] = jnp.sum(received[...], axis=0) * (1.0 / 512.0)
    swap = remote(total.at[0], total.at[1], send.at[first + 1], recv.at[first + 1], sibling)
    swap.start()
    swap.wait()
    total[2] = total[0] + total[1]


def sums_gather(place, send, recv, sums, received, total, totals, first, chip, core):
    whole = totals.reshape(CHIPS, 8, 128)

    def act(device):
        remote(total.at[2], whole.at[chip], send.at[first + 2], recv.at[first + 2], device + core).start()

    for_chips(place, act)
    pltpu.make_async_copy(total.at[2], whole.at[chip], recv.at[first + 2]).start()


def kernel(
    pair_hbm,
    cot_hbm,
    in_gain_hbm,
    w_in_hbm,
    out_gain_hbm,
    w_out_hbm,
    next_hbm,
    back_hbm,
    early_totals,
    late_totals,
    next_ref,
    back_ref,
    pair_ref,
    cot_ref,
    in_gain_ref,
    w_in_ref,
    out_gain_ref,
    w_out_ref,
    w_in_t,
    w_out_t,
    in_gain_t,
    out_gain_t,
    perm,
    rows_perm,
    rows_perm_t,
    pair_t,
    cot_t,
    hat,
    rstd,
    normed,
    left_a,
    left_b,
    right_a,
    right_b,
    gate,
    proj_cot,
    scaled,
    tri_hat,
    tri_normed,
    spread,
    l_out,
    l_in,
    r_out,
    r_in,
    left,
    right_raw,
    right,
    tri_out,
    tri_in,
    tc_out,
    tc_in,
    tc,
    tc_t,
    lc_out,
    lc_in,
    rc_out,
    rc_in,
    project_cot,
    early_sums,
    early_in,
    early_total,
    late_sums,
    late_in,
    late_total,
    load,
    store,
    send,
    recv,
):
    *place, core = parts()
    me = lax.axis_index("row") * 16 + lax.axis_index("col")
    chip = me // 2
    sibling = me + 1 - 2 * core
    loads = [
        pltpu.make_async_copy(src, dst, load.at[n])
        for n, (src, dst) in enumerate(
            (
                (pair_hbm, pair_ref),
                (w_in_hbm, w_in_ref),
                (in_gain_hbm, in_gain_ref),
                (cot_hbm, cot_ref),
                (w_out_hbm, w_out_ref),
                (out_gain_hbm, out_gain_ref),
            )
        )
    ]
    for copy in loads:
        copy.start()
    greet(place, sibling)

    for copy in loads[:3]:
        copy.wait()
    for n in range(5):
        w_in_t[block(n), :] = w_in_ref[:, block(n)].T
    in_gain_t[...] = jnp.broadcast_to(in_gain_ref[...], (128, 128)).T

    def project(chunk, carry):
        cells = cells_of(chunk)
        x = pair_ref[cells, :].astype(F32).T
        pair_t[:, cells] = x
        center = x - jnp.mean(x, axis=0, keepdims=True)
        inverse = lax.rsqrt(jnp.mean(center * center, axis=0, keepdims=True) + EPSILON)
        x_hat = center * inverse
        hat[:, cells] = x_hat
        rstd[:, cells] = inverse
        y = (x_hat * in_gain_t[:, :1]).astype(BF16)
        normed[:, cells] = y
        for side, (keep_a, keep_b) in enumerate(((left_a, left_b), (right_a, right_b))):
            both = matmul(w_in_t[pl.ds(side * 256, 256), :], y)
            sig = jax.nn.sigmoid(both[:128])
            act = sig * both[128:]
            keep_b[:, cells] = sig
            keep_a[:, cells] = act * (1.0 - sig)
            put_tiles(spread, side * 2048, chunk, act)
        return carry

    lax.fori_loop(0, STEPS, project, 0, unroll=True)
    r_out[...] = spread[pl.ds(2048, 2048), :].astype(BF16).reshape(128, 16, 128)
    pl.semaphore_wait(pltpu.get_barrier_semaphore(), DEVICES - 1)
    right_way = (r_out, r_in, send.at[0], recv.at[0], me)
    left_way = (l_out, l_in, send.at[1], recv.at[1], me)
    send_to(0, place, *right_way)
    l_out[...] = spread[pl.ds(0, 2048), :].astype(BF16).reshape(128, 16, 128)
    send_to(0, place, *left_way)
    send_to(1, place, *right_way)
    send_near(sibling, *right_way)
    send_to(1, place, *left_way)
    send_near(sibling, *left_way)

    a = lax.broadcasted_iota(jnp.int32, (512, 512), 0)
    b = lax.broadcasted_iota(jnp.int32, (512, 512), 1)
    swapped = ((a // 32) % 4) * 128 + (a // 128) * 32 + a % 32
    perm[...] = jnp.where(swapped == b, 1.0, 0.0).astype(BF16)
    rows_perm[...] = jnp.where((a % 4) * 128 + a // 4 == b, 1.0, 0.0).astype(BF16)
    rows_perm_t[...] = jnp.where((b % 4) * 128 + b // 4 == a, 1.0, 0.0).astype(BF16)
    for copy in loads[3:]:
        copy.wait()
    w_out_t[...] = w_out_ref[...].T
    out_gain_t[...] = jnp.broadcast_to(out_gain_ref[...], (128, 128)).T

    def upstream(chunk, carry):
        cells = cells_of(chunk)
        sig = jax.nn.sigmoid(matmul(w_in_t[pl.ds(512, 128), :], normed[:, cells]))
        gate[:, cells] = sig
        up = cot_ref[cells, :].astype(F32).T
        cot_t[:, cells] = up
        back = (up * sig).astype(BF16)
        proj_cot[:, cells] = back
        scaled[:, cells] = matmul(w_out_ref[...], back) * out_gain_t[:, :1]
        return carry

    lax.fori_loop(0, STEPS, upstream, 0, unroll=True)

    wait_all(r_in, recv.at[0])
    gather_matrix(r_in.reshape(8, 16, 16, 128), perm, right_raw)
    right[...] = matmul(rows_perm[...], right_raw[...]).astype(BF16)
    wait_all(l_in, recv.at[1])
    gather_matrix(l_in.reshape(8, 16, 16, 128), perm, left)
    scatter_matrix(matmul_nt(left[...], right[...]), perm, tri_out.reshape(8, 16, 16, 128))
    way = (tri_out, tri_in, send.at[2], recv.at[2], me)
    send_to(0, place, *way)
    send_to(1, place, *way)
    send_near(sibling, *way)
    wait_all(tri_in, recv.at[2])

    spread[pl.ds(0, 2048), :] = tri_in[...].reshape(2048, 128).astype(F32)

    def middle(chunk, carry):
        cells = cells_of(chunk)
        x = get_tiles(spread, 0, chunk)
        center = x - jnp.mean(x, axis=0, keepdims=True)
        inverse = lax.rsqrt(jnp.mean(center * center, axis=0, keepdims=True) + EPSILON)
        x_hat = center * inverse
        tri_hat[:, cells] = x_hat
        grad = scaled[:, cells]
        mean = jnp.mean(grad, axis=0, keepdims=True)
        along = jnp.mean(grad * x_hat, axis=0, keepdims=True)
        put_tiles(spread, 2048, chunk, inverse * (grad - mean - x_hat * along))
        return carry

    lax.fori_loop(0, STEPS, middle, 0, unroll=True)
    tc_out[...] = spread[pl.ds(2048, 2048), :].astype(BF16).reshape(128, 16, 128)
    way = (tc_out, tc_in, send.at[3], recv.at[3], me)
    send_to(0, place, *way)
    send_to(1, place, *way)
    send_near(sibling, *way)

    def update(chunk, carry):
        cells = cells_of(chunk)
        y = (tri_hat[:, cells] * out_gain_t[:, :1]).astype(BF16)
        tri_normed[:, cells] = y
        projected = matmul(w_out_t[...], y)
        sig = gate[:, cells]
        next_ref[cells, :] = (pair_t[:, cells] + sig * projected).T.astype(BF16)
        project_cot[pl.ds(512, 128), cells] = (
            cot_t[:, cells] * projected * sig * (1.0 - sig)
        ).astype(BF16)
        return carry

    lax.fori_loop(0, STEPS, update, 0, unroll=True)

    early = (early_sums, early_in, early_total, early_totals, 6, chip, core)
    late = (late_sums, late_in, late_total, late_totals, 9, chip, core)
    w_out_sum = matmul_nt(tri_normed[...], proj_cot[...])
    put_row(early_sums, 0, matmul_nt(normed[...], project_cot[block(4), :]))
    for n in (1, 2, 3):
        put_row(early_sums, n, w_out_sum)
    sums_scatter(place, send, recv, *early)
    next_copy = pltpu.make_async_copy(next_ref, next_hbm, store.at[0])
    next_copy.start()
    wait_all(tc_in, recv.at[3])

    gather_matrix(tc_in.reshape(8, 16, 16, 128), perm, tc)
    scatter_matrix(matmul(tc[...], right[...]), perm, lc_out.reshape(8, 16, 16, 128))
    left_way = (lc_out, lc_in, send.at[4], recv.at[4], me)
    send_to(0, place, *left_way)
    tc_t[...] = matmul_nt(rows_perm_t[...], tc[...]).astype(BF16)
    scatter_matrix(matmul(tc_t[...], left[...]), perm, rc_out.reshape(8, 16, 16, 128))
    right_way = (rc_out, rc_in, send.at[5], recv.at[5], me)
    send_to(0, place, *right_way)
    send_to(1, place, *left_way)
    send_near(sibling, *left_way)
    send_to(1, place, *right_way)
    send_near(sibling, *right_way)

    sums_add(sibling, send, recv, *early)

    for side, (got, keep_a, keep_b) in enumerate(((lc_in, left_a, left_b), (rc_in, right_a, right_b))):
        wait_all(got, recv.at[4 + side])
        spread[pl.ds(side * 2048, 2048), :] = got[...].reshape(2048, 128).astype(F32)

        def products(chunk, carry):
            cells = cells_of(chunk)
            grad = get_tiles(spread, side * 2048, chunk)
            project_cot[pl.ds(side * 256, 128), cells] = (grad * keep_a[:, cells]).astype(BF16)
            project_cot[pl.ds(side * 256 + 128, 128), cells] = (grad * keep_b[:, cells]).astype(BF16)
            return carry

        lax.fori_loop(0, STEPS, products, 0, unroll=True)
        part = matmul_nt(normed[...], project_cot[pl.ds(side * 256, 256), :])
        put_row(late_sums, 2 * side, part[:, :128])
        put_row(late_sums, 2 * side + 1, part[:, 128:])

    sums_scatter(place, send, recv, *late)
    sums_gather(place, send, recv, *early)

    def finish(chunk, carry):
        cells = cells_of(chunk)
        grad = matmul(w_in_ref[...], project_cot[:, cells]) * in_gain_t[:, :1]
        x_hat = hat[:, cells]
        mean = jnp.mean(grad, axis=0, keepdims=True)
        along = jnp.mean(grad * x_hat, axis=0, keepdims=True)
        back = rstd[:, cells] * (grad - mean - x_hat * along)
        back_ref[cells, :] = (cot_t[:, cells] + back).T.astype(BF16)
        return carry

    lax.fori_loop(0, STEPS, finish, 0, unroll=True)
    back_copy = pltpu.make_async_copy(back_ref, back_hbm, store.at[1])
    back_copy.start()
    sums_add(sibling, send, recv, *late)
    sums_gather(place, send, recv, *late)
    wait_all(early_totals, recv.at[8])
    wait_all(late_totals, recv.at[11])

    next_copy.wait()
    back_copy.wait()
    wait_sent(r_out, send.at[0])
    wait_sent(l_out, send.at[1])
    wait_sent(tri_out, send.at[2])
    wait_sent(tc_out, send.at[3])
    wait_sent(lc_out, send.at[4])
    wait_sent(rc_out, send.at[5])
    for n in (6, 8, 9, 11):
        wait_sent(early_in, send.at[n])


def deliver(
    next_hbm,
    back_hbm,
    early_hbm,
    late_hbm,
    in_gain_hbm,
    w_in_hbm,
    out_gain_hbm,
    w_out_hbm,
    next_out,
    back_out,
    in_gain_grad_out,
    w_in_grad_out,
    out_gain_grad_out,
    w_out_grad_out,
    next_ref,
    back_ref,
    early,
    late,
    in_gain,
    w_in,
    out_gain,
    w_out,
    in_gain_grad,
    w_in_grad,
    out_gain_grad,
    w_out_grad,
    load,
    store,
):
    sources = (early_hbm, late_hbm, in_gain_hbm, w_in_hbm, out_gain_hbm, w_out_hbm, next_hbm, back_hbm)
    holds = (early, late, in_gain, w_in, out_gain, w_out, next_ref, back_ref)
    loads = [pltpu.make_async_copy(src, dst, load.at[n]) for n, (src, dst) in enumerate(zip(sources, holds))]
    results = (next_ref, back_ref, in_gain_grad, w_in_grad, out_gain_grad, w_out_grad)
    places = (next_out, back_out, in_gain_grad_out, w_in_grad_out, out_gain_grad_out, w_out_grad_out)
    stores = [pltpu.make_async_copy(src, dst, store.at[n]) for n, (src, dst) in enumerate(zip(results, places))]
    for copy in loads:
        copy.start()
    for n in (0, 1):
        loads[6 + n].wait()
        stores[n].start()
    for copy in loads[:6]:
        copy.wait()
    along = jnp.zeros((128, 128), F32)
    for n in range(5):
        part = get_row(early, 0) if n == 4 else get_row(late, n)
        w_in_grad[:, block(n)] = part
        along += part * w_in[:, block(n)].astype(F32)
    stores[3].start()
    part = get_row(early, 1)
    w_out_grad[...] = part
    stores[5].start()
    in_gain_grad[...] = jnp.sum(along.T, axis=0, keepdims=True) / in_gain[...]
    along = part * w_out[...].astype(F32)
    out_gain_grad[...] = jnp.sum(along.T, axis=0, keepdims=True) / out_gain[...]
    stores[2].start()
    stores[4].start()
    for copy in stores:
        copy.wait()


def on_device(pair, cotangent, in_gain, w_in, out_gain, w_out):
    hbm = pl.BlockSpec(memory_space=pltpu.HBM)

    def bf(*shape):
        return pltpu.VMEM(shape, BF16)

    def fl(*shape):
        return pltpu.VMEM(shape, F32)

    scratch = [
        bf(2048, 128),
        bf(2048, 128),
        bf(2048, 128),
        bf(2048, 128),
        fl(1, 128),
        bf(128, 640),
        fl(1, 128),
        bf(128, 128),
        bf(640, 128),
        bf(128, 128),
        fl(128, 128),
        fl(128, 128),
        bf(512, 512),
        bf(512, 512),
        bf(512, 512),
        fl(128, 2048),
        fl(128, 2048),
        fl(128, 2048),
        fl(1, 2048),
        bf(128, 2048),
        fl(128, 2048),
        fl(128, 2048),
        fl(128, 2048),
        fl(128, 2048),
        fl(128, 2048),
        bf(128, 2048),
        fl(128, 2048),
        fl(128, 2048),
        bf(128, 2048),
        fl(4096, 128),
        bf(128, 16, 128),
        bf(128, 16, 128),
        bf(128, 16, 128),
        bf(128, 16, 128),
        bf(512, 512),
        bf(512, 512),
        bf(512, 512),
        bf(128, 16, 128),
        bf(128, 16, 128),
        bf(128, 16, 128),
        bf(128, 16, 128),
        bf(512, 512),
        bf(512, 512),
        bf(128, 16, 128),
        bf(128, 16, 128),
        bf(128, 16, 128),
        bf(128, 16, 128),
        bf(640, 2048),
        fl(512, 128),
        fl(64, 8, 128),
        fl(3, 8, 128),
        fl(512, 128),
        fl(64, 8, 128),
        fl(3, 8, 128),
        pltpu.SemaphoreType.DMA((6,)),
        pltpu.SemaphoreType.DMA((2,)),
        pltpu.SemaphoreType.DMA((12,)),
        pltpu.SemaphoreType.DMA((12,)),
    ]
    shapes = [
        jax.ShapeDtypeStruct((CELLS, CH), BF16),
        jax.ShapeDtypeStruct((CELLS, CH), BF16),
        jax.ShapeDtypeStruct((1, CH), F32),
        jax.ShapeDtypeStruct((CH, 640), F32),
        jax.ShapeDtypeStruct((1, CH), F32),
        jax.ShapeDtypeStruct((CH, CH), F32),
    ]
    params = (in_gain.reshape(1, CH), w_in, out_gain.reshape(1, CH), w_out)
    sums_shape = jax.ShapeDtypeStruct((512, 128), F32)
    results = pl.pallas_call(
        kernel,
        out_shape=shapes[:2] + [sums_shape] * 2,
        in_specs=[hbm] * 6,
        out_specs=[hbm] * 4,
        scratch_shapes=scratch,
        compiler_params=pltpu.CompilerParams(
            collective_id=0, has_side_effects=True, vmem_limit_bytes=VMEM_BYTES
        ),
        name="triangle_update",
    )(pair.reshape(CELLS, CH), cotangent.reshape(CELLS, CH), *params)
    pair_next, pair_back, in_gain_grad, w_in_grad, out_gain_grad, w_out_grad = pl.pallas_call(
        deliver,
        out_shape=shapes,
        in_specs=[hbm] * 8,
        out_specs=[hbm] * 6,
        scratch_shapes=[
            bf(CELLS, CH),
            bf(CELLS, CH),
            fl(512, 128),
            fl(512, 128),
            fl(1, CH),
            bf(CH, 640),
            fl(1, CH),
            bf(CH, CH),
            fl(1, CH),
            fl(CH, 640),
            fl(1, CH),
            fl(CH, CH),
            pltpu.SemaphoreType.DMA((8,)),
            pltpu.SemaphoreType.DMA((6,)),
        ],
        compiler_params=pltpu.CompilerParams(vmem_limit_bytes=VMEM_BYTES),
        name="deliver",
    )(*results, *params)
    return (
        pair_next.reshape(64, 32, CH),
        pair_back.reshape(64, 32, CH),
        in_gain_grad.reshape(CH),
        w_in_grad,
        out_gain_grad.reshape(CH),
        w_out_grad,
    )


def solution(mesh):
    in_specs = (P("row", "col", None), P("row", "col", None), P(), P(), P(), P())
    out_specs = (P("row", "col", None), P("row", "col", None), P(), P(), P(), P())
    return jax.shard_map(
        on_device, mesh=mesh, in_specs=in_specs, out_specs=out_specs, check_vma=False
    )
```

```python
import itertools

import jax
import jax.numpy as jnp
from jax import lax
from jax.experimental import pallas as pl
from jax.experimental.pallas import tpu as pltpu
from jax.sharding import PartitionSpec as P

EPSILON = 1e-05
LOGICAL = pl.DeviceIdType.LOGICAL
DEVICES = 128
CHIPS = 64
CH = 128
CELLS = 2048
CHUNK = 256
TILES = CHUNK // 128
STEPS = CELLS // CHUNK
VMEM_BYTES = 63 * 2**20
F32 = jnp.float32
BF16 = jnp.bfloat16
HOPS = sorted(itertools.product((0, 1, 2), repeat=3), key=lambda hops: (-sum(hops), hops))[:-1]


def matmul(a, b):
    return jnp.dot(a, b, preferred_element_type=F32)


def matmul_nt(a, b):
    return lax.dot_general(a, b, (((1,), (1,)), ((), ())), preferred_element_type=F32)


def parts():
    row, col = lax.axis_index("row"), lax.axis_index("col")
    x, y, z, core = (row // 4) * 2 + col // 8, (col // 2) % 4, row % 4, col % 2
    xs = [((x + d) % 4 // 2) * 64 + ((x + d) % 4 % 2) * 8 for d in range(4)]
    ys = [((y + d) % 4) * 2 for d in range(4)]
    zs = [((z + d) % 4) * 16 for d in range(4)]
    return xs, ys, zs, core


def for_chips(place, act):
    for hops in HOPS:
        ways = [(1, 3) if h == 1 else (h,) for h in hops]
        for dx, dy, dz in itertools.product(*ways):
            act(place[0][dx] + place[1][dy] + place[2][dz])


def greet(place, sibling):
    barrier = pltpu.get_barrier_semaphore()

    def signal(device):
        pl.semaphore_signal(barrier, inc=1, device_id=device, device_id_type=LOGICAL)

    def act(device):
        signal(device)
        signal(device + 1)

    for_chips(place, act)
    signal(sibling)


def remote(src, dst, send, recv, device):
    return pltpu.make_async_remote_copy(
        src_ref=src, dst_ref=dst, send_sem=send, recv_sem=recv, device_id=device, device_id_type=LOGICAL
    )


def send_to(core, place, src, dst, send, recv, me):
    def act(device):
        remote(src.at[device + core], dst.at[me], send, recv, device + core).start()

    for_chips(place, act)


def send_near(sibling, src, dst, send, recv, me):
    remote(src.at[sibling], dst.at[me], send, recv, sibling).start()
    pltpu.make_async_copy(src.at[me], dst.at[me], recv).start()


def wait_all(ref, sem):
    pltpu.make_async_copy(ref, ref, sem).wait()


def wait_sent(ref, sem):
    part = ref.at[pl.ds(0, ref.shape[0] - 1)]
    pltpu.make_async_copy(part, part, sem).wait()


def block(index):
    return pl.ds(index * 128, 128)


def cells_of(chunk):
    return pl.ds(pl.multiple_of(chunk * CHUNK, CHUNK), CHUNK)


def gather_matrix(received, perm, whole):
    rows = [
        jnp.concatenate([received[:, q_hi * 4 + q_lo].reshape(128, 128) for q_lo in range(4)], axis=1)
        for q_hi in range(4)
    ]
    moved = matmul(jnp.concatenate(rows, axis=0), perm[...]).astype(BF16)
    for q_hi in range(4):
        for i_lo in range(4):
            whole[block(i_lo), block(q_hi)] = tile(moved, q_hi, i_lo)


def scatter_matrix(whole, perm, outgoing):
    whole = whole.astype(BF16)
    rows = [
        jnp.concatenate([tile(whole, i_lo, q_hi) for i_lo in range(4)], axis=1) for q_hi in range(4)
    ]
    moved = matmul(jnp.concatenate(rows, axis=0), perm[...]).astype(BF16)
    for q_hi in range(4):
        for q_lo in range(4):
            outgoing[:, q_hi * 4 + q_lo] = tile(moved, q_hi, q_lo).reshape(8, 16, 128)


def tile(value, i, j):
    return value[i * 128 : (i + 1) * 128, j * 128 : (j + 1) * 128]


def put_tiles(spread, base, chunk, value):
    for t in range(TILES):
        spread[pl.ds(base + chunk * TILES + t, 128, stride=16), :] = value[:, t * 128 : (t + 1) * 128]


def get_tiles(spread, base, chunk):
    tiles = [spread[pl.ds(base + chunk * TILES + t, 128, stride=16), :] for t in range(TILES)]
    return jnp.concatenate(tiles, axis=1)


def put_row(rows, index, value):
    rows[pl.ds(index, 128, stride=4), :] = value


def get_row(rows, index):
    return rows[pl.ds(index, 128, stride=4), :]


def sums_scatter(place, send, recv, sums, received, total, totals, first, me):
    tiles = sums.reshape(CHIPS, 8, 128)
    own = tiles.at[me // 2]

    def act(device):
        chip = device // 2
        remote(
            tiles.at[chip], received.at[me], send.at[first], recv.at[first], device + chip % 2
        ).start()

    for_chips(place, act)

    @pl.when(me // 2 % 2 == me % 2)
    def _():
        pltpu.make_async_copy(own, received.at[me], recv.at[first]).start()

    @pl.when(me // 2 % 2 != me % 2)
    def _():
        device = me + 1 - 2 * (me % 2)
        remote(own, received.at[me], send.at[first + 1], recv.at[first], device).start()


def sums_gather(place, send, recv, sums, received, total, totals, first, me):
    whole = totals.reshape(CHIPS, 8, 128)
    chip = me // 2

    @pl.when(chip % 2 == me % 2)
    def _():
        wait_all(received, recv.at[first])
        total[...] = jnp.sum(received[...], axis=0) * (1.0 / 512.0)

        def act(device):
            for core in range(2):
                remote(
                    total, whole.at[chip], send.at[first + 2], recv.at[first + 2], device + core
                ).start()

        for_chips(place, act)
        sibling = me + 1 - 2 * (me % 2)
        remote(total, whole.at[chip], send.at[first + 2], recv.at[first + 2], sibling).start()
        pltpu.make_async_copy(total, whole.at[chip], recv.at[first + 2]).start()


def sums_sent(send, sums, received, total, totals, first, me):
    tiles = sums.reshape(CHIPS, 8, 128)
    wait_sent(tiles, send.at[first])

    @pl.when(me // 2 % 2 == me % 2)
    def _():
        wait_sent(received, send.at[first + 2])

    @pl.when(me // 2 % 2 != me % 2)
    def _():
        wait_all(total, send.at[first + 1])


def kernel(
    pair_hbm,
    cot_hbm,
    in_gain_hbm,
    w_in_hbm,
    out_gain_hbm,
    w_out_hbm,
    next_hbm,
    back_hbm,
    early_totals,
    late_totals,
    next_ref,
    back_ref,
    pair_ref,
    cot_ref,
    in_gain_ref,
    w_in_ref,
    out_gain_ref,
    w_out_ref,
    w_in_t,
    w_out_t,
    in_gain_t,
    out_gain_t,
    perm,
    rows_perm,
    rows_perm_t,
    pair_t,
    cot_t,
    hat,
    rstd,
    normed,
    left_a,
    left_b,
    right_a,
    right_b,
    gate,
    proj_cot,
    scaled,
    tri_hat,
    tri_normed,
    spread,
    l_out,
    l_in,
    r_out,
    r_in,
    left,
    right_raw,
    right,
    tri_out,
    tri_in,
    tc_out,
    tc_in,
    tc,
    tc_t,
    lc_out,
    lc_in,
    rc_out,
    rc_in,
    project_cot,
    early_sums,
    early_in,
    early_total,
    late_sums,
    late_in,
    late_total,
    load,
    store,
    send,
    recv,
):
    *place, core = parts()
    me = lax.axis_index("row") * 16 + lax.axis_index("col")
    sibling = me + 1 - 2 * core
    loads = [
        pltpu.make_async_copy(src, dst, load.at[n])
        for n, (src, dst) in enumerate(
            (
                (pair_hbm, pair_ref),
                (w_in_hbm, w_in_ref),
                (in_gain_hbm, in_gain_ref),
                (cot_hbm, cot_ref),
                (w_out_hbm, w_out_ref),
                (out_gain_hbm, out_gain_ref),
            )
        )
    ]
    for copy in loads:
        copy.start()
    greet(place, sibling)

    for copy in loads[:3]:
        copy.wait()
    for n in range(5):
        w_in_t[block(n), :] = w_in_ref[:, block(n)].T
    in_gain_t[...] = jnp.broadcast_to(in_gain_ref[...], (128, 128)).T

    def project(chunk, carry):
        cells = cells_of(chunk)
        x = pair_ref[cells, :].astype(F32).T
        pair_t[:, cells] = x
        center = x - jnp.mean(x, axis=0, keepdims=True)
        inverse = lax.rsqrt(jnp.mean(center * center, axis=0, keepdims=True) + EPSILON)
        x_hat = center * inverse
        hat[:, cells] = x_hat
        rstd[:, cells] = inverse
        y = (x_hat * in_gain_t[:, :1]).astype(BF16)
        normed[:, cells] = y
        for side, (keep_a, keep_b) in enumerate(((left_a, left_b), (right_a, right_b))):
            both = matmul(w_in_t[pl.ds(side * 256, 256), :], y)
            sig = jax.nn.sigmoid(both[:128])
            act = sig * both[128:]
            keep_b[:, cells] = sig
            keep_a[:, cells] = act * (1.0 - sig)
            put_tiles(spread, side * 2048, chunk, act)
        return carry

    lax.fori_loop(0, STEPS, project, 0, unroll=4)
    r_out[...] = spread[pl.ds(2048, 2048), :].astype(BF16).reshape(128, 16, 128)
    pl.semaphore_wait(pltpu.get_barrier_semaphore(), DEVICES - 1)
    right_way = (r_out, r_in, send.at[0], recv.at[0], me)
    left_way = (l_out, l_in, send.at[1], recv.at[1], me)
    send_to(0, place, *right_way)
    l_out[...] = spread[pl.ds(0, 2048), :].astype(BF16).reshape(128, 16, 128)
    send_to(0, place, *left_way)
    send_to(1, place, *right_way)
    send_near(sibling, *right_way)
    send_to(1, place, *left_way)
    send_near(sibling, *left_way)

    a = lax.broadcasted_iota(jnp.int32, (512, 512), 0)
    b = lax.broadcasted_iota(jnp.int32, (512, 512), 1)
    swapped = ((a // 32) % 4) * 128 + (a // 128) * 32 + a % 32
    perm[...] = jnp.where(swapped == b, 1.0, 0.0).astype(BF16)
    rows_perm[...] = jnp.where((a % 4) * 128 + a // 4 == b, 1.0, 0.0).astype(BF16)
    rows_perm_t[...] = jnp.where((b % 4) * 128 + b // 4 == a, 1.0, 0.0).astype(BF16)
    for copy in loads[3:]:
        copy.wait()
    w_out_t[...] = w_out_ref[...].T
    out_gain_t[...] = jnp.broadcast_to(out_gain_ref[...], (128, 128)).T

    def upstream(chunk, carry):
        cells = cells_of(chunk)
        sig = jax.nn.sigmoid(matmul(w_in_t[pl.ds(512, 128), :], normed[:, cells]))
        gate[:, cells] = sig
        up = cot_ref[cells, :].astype(F32).T
        cot_t[:, cells] = up
        back = (up * sig).astype(BF16)
        proj_cot[:, cells] = back
        scaled[:, cells] = matmul(w_out_ref[...], back) * out_gain_t[:, :1]
        return carry

    lax.fori_loop(0, STEPS, upstream, 0)

    wait_all(r_in, recv.at[0])
    gather_matrix(r_in.reshape(8, 16, 16, 128), perm, right_raw)
    right[...] = matmul(rows_perm[...], right_raw[...]).astype(BF16)
    wait_all(l_in, recv.at[1])
    gather_matrix(l_in.reshape(8, 16, 16, 128), perm, left)
    scatter_matrix(matmul_nt(left[...], right[...]), perm, tri_out.reshape(8, 16, 16, 128))
    way = (tri_out, tri_in, send.at[2], recv.at[2], me)
    send_to(0, place, *way)
    send_to(1, place, *way)
    send_near(sibling, *way)
    wait_all(tri_in, recv.at[2])

    spread[pl.ds(0, 2048), :] = tri_in[...].reshape(2048, 128).astype(F32)

    def middle(chunk, carry):
        cells = cells_of(chunk)
        x = get_tiles(spread, 0, chunk)
        center = x - jnp.mean(x, axis=0, keepdims=True)
        inverse = lax.rsqrt(jnp.mean(center * center, axis=0, keepdims=True) + EPSILON)
        x_hat = center * inverse
        tri_hat[:, cells] = x_hat
        grad = scaled[:, cells]
        mean = jnp.mean(grad, axis=0, keepdims=True)
        along = jnp.mean(grad * x_hat, axis=0, keepdims=True)
        put_tiles(spread, 2048, chunk, inverse * (grad - mean - x_hat * along))
        return carry

    lax.fori_loop(0, STEPS, middle, 0, unroll=True)
    tc_out[...] = spread[pl.ds(2048, 2048), :].astype(BF16).reshape(128, 16, 128)
    way = (tc_out, tc_in, send.at[3], recv.at[3], me)
    send_to(0, place, *way)
    send_to(1, place, *way)
    send_near(sibling, *way)

    def update(chunk, carry):
        cells = cells_of(chunk)
        y = (tri_hat[:, cells] * out_gain_t[:, :1]).astype(BF16)
        tri_normed[:, cells] = y
        projected = matmul(w_out_t[...], y)
        sig = gate[:, cells]
        next_ref[cells, :] = (pair_t[:, cells] + sig * projected).T.astype(BF16)
        project_cot[pl.ds(512, 128), cells] = (
            cot_t[:, cells] * projected * sig * (1.0 - sig)
        ).astype(BF16)
        return carry

    lax.fori_loop(0, STEPS, update, 0)

    early = (early_sums, early_in, early_total, early_totals, 6, me)
    late = (late_sums, late_in, late_total, late_totals, 9, me)
    w_out_sum = matmul_nt(tri_normed[...], proj_cot[...])
    put_row(early_sums, 0, matmul_nt(normed[...], project_cot[block(4), :]))
    for n in (1, 2, 3):
        put_row(early_sums, n, w_out_sum)
    sums_scatter(place, send, recv, *early)
    next_copy = pltpu.make_async_copy(next_ref, next_hbm, store.at[0])
    next_copy.start()
    wait_all(tc_in, recv.at[3])

    gather_matrix(tc_in.reshape(8, 16, 16, 128), perm, tc)
    scatter_matrix(matmul(tc[...], right[...]), perm, lc_out.reshape(8, 16, 16, 128))
    left_way = (lc_out, lc_in, send.at[4], recv.at[4], me)
    send_to(0, place, *left_way)
    tc_t[...] = matmul_nt(rows_perm_t[...], tc[...]).astype(BF16)
    scatter_matrix(matmul(tc_t[...], left[...]), perm, rc_out.reshape(8, 16, 16, 128))
    right_way = (rc_out, rc_in, send.at[5], recv.at[5], me)
    send_to(0, place, *right_way)
    send_to(1, place, *left_way)
    send_near(sibling, *left_way)
    send_to(1, place, *right_way)
    send_near(sibling, *right_way)

    for side, (got, keep_a, keep_b) in enumerate(((lc_in, left_a, left_b), (rc_in, right_a, right_b))):
        wait_all(got, recv.at[4 + side])
        spread[pl.ds(side * 2048, 2048), :] = got[...].reshape(2048, 128).astype(F32)

        def products(chunk, carry):
            cells = cells_of(chunk)
            grad = get_tiles(spread, side * 2048, chunk)
            project_cot[pl.ds(side * 256, 128), cells] = (grad * keep_a[:, cells]).astype(BF16)
            project_cot[pl.ds(side * 256 + 128, 128), cells] = (grad * keep_b[:, cells]).astype(BF16)
            return carry

        lax.fori_loop(0, STEPS, products, 0, unroll=True)
        part = matmul_nt(normed[...], project_cot[pl.ds(side * 256, 256), :])
        put_row(late_sums, 2 * side, part[:, :128])
        put_row(late_sums, 2 * side + 1, part[:, 128:])

    sums_scatter(place, send, recv, *late)
    sums_gather(place, send, recv, *early)

    def finish(chunk, carry):
        cells = cells_of(chunk)
        grad = matmul(w_in_ref[...], project_cot[:, cells]) * in_gain_t[:, :1]
        x_hat = hat[:, cells]
        mean = jnp.mean(grad, axis=0, keepdims=True)
        along = jnp.mean(grad * x_hat, axis=0, keepdims=True)
        back = rstd[:, cells] * (grad - mean - x_hat * along)
        back_ref[cells, :] = (cot_t[:, cells] + back).T.astype(BF16)
        return carry

    lax.fori_loop(0, STEPS, finish, 0, unroll=2)
    back_copy = pltpu.make_async_copy(back_ref, back_hbm, store.at[1])
    back_copy.start()
    sums_gather(place, send, recv, *late)
    wait_all(early_totals, recv.at[8])
    wait_all(late_totals, recv.at[11])

    next_copy.wait()
    back_copy.wait()
    wait_sent(r_out, send.at[0])
    wait_sent(l_out, send.at[1])
    wait_sent(tri_out, send.at[2])
    wait_sent(tc_out, send.at[3])
    wait_sent(lc_out, send.at[4])
    wait_sent(rc_out, send.at[5])
    sums_sent(send, *early)
    sums_sent(send, *late)


def deliver(
    next_hbm,
    back_hbm,
    early_hbm,
    late_hbm,
    in_gain_hbm,
    w_in_hbm,
    out_gain_hbm,
    w_out_hbm,
    next_out,
    back_out,
    in_gain_grad_out,
    w_in_grad_out,
    out_gain_grad_out,
    w_out_grad_out,
    next_ref,
    back_ref,
    early,
    late,
    in_gain,
    w_in,
    out_gain,
    w_out,
    in_gain_grad,
    w_in_grad,
    out_gain_grad,
    w_out_grad,
    load,
    store,
):
    sources = (early_hbm, late_hbm, in_gain_hbm, w_in_hbm, out_gain_hbm, w_out_hbm, next_hbm, back_hbm)
    holds = (early, late, in_gain, w_in, out_gain, w_out, next_ref, back_ref)
    loads = [pltpu.make_async_copy(src, dst, load.at[n]) for n, (src, dst) in enumerate(zip(sources, holds))]
    results = (next_ref, back_ref, in_gain_grad, w_in_grad, out_gain_grad, w_out_grad)
    places = (next_out, back_out, in_gain_grad_out, w_in_grad_out, out_gain_grad_out, w_out_grad_out)
    stores = [pltpu.make_async_copy(src, dst, store.at[n]) for n, (src, dst) in enumerate(zip(results, places))]
    for copy in loads:
        copy.start()
    for n in (0, 1):
        loads[6 + n].wait()
        stores[n].start()
    for copy in loads[:6]:
        copy.wait()
    along = jnp.zeros((128, 128), F32)
    for n in range(5):
        part = get_row(early, 0) if n == 4 else get_row(late, n)
        w_in_grad[:, block(n)] = part
        along += part * w_in[:, block(n)].astype(F32)
    stores[3].start()
    part = get_row(early, 1)
    w_out_grad[...] = part
    stores[5].start()
    in_gain_grad[...] = jnp.sum(along.T, axis=0, keepdims=True) / in_gain[...]
    along = part * w_out[...].astype(F32)
    out_gain_grad[...] = jnp.sum(along.T, axis=0, keepdims=True) / out_gain[...]
    stores[2].start()
    stores[4].start()
    for copy in stores:
        copy.wait()


def on_device(pair, cotangent, in_gain, w_in, out_gain, w_out):
    hbm = pl.BlockSpec(memory_space=pltpu.HBM)

    def bf(*shape):
        return pltpu.VMEM(shape, BF16)

    def fl(*shape):
        return pltpu.VMEM(shape, F32)

    scratch = [
        bf(2048, 128),
        bf(2048, 128),
        bf(2048, 128),
        bf(2048, 128),
        fl(1, 128),
        bf(128, 640),
        fl(1, 128),
        bf(128, 128),
        bf(640, 128),
        bf(128, 128),
        fl(128, 128),
        fl(128, 128),
        bf(512, 512),
        bf(512, 512),
        bf(512, 512),
        fl(128, 2048),
        fl(128, 2048),
        fl(128, 2048),
        fl(1, 2048),
        bf(128, 2048),
        fl(128, 2048),
        fl(128, 2048),
        fl(128, 2048),
        fl(128, 2048),
        fl(128, 2048),
        bf(128, 2048),
        fl(128, 2048),
        fl(128, 2048),
        bf(128, 2048),
        fl(4096, 128),
        bf(128, 16, 128),
        bf(128, 16, 128),
        bf(128, 16, 128),
        bf(128, 16, 128),
        bf(512, 512),
        bf(512, 512),
        bf(512, 512),
        bf(128, 16, 128),
        bf(128, 16, 128),
        bf(128, 16, 128),
        bf(128, 16, 128),
        bf(512, 512),
        bf(512, 512),
        bf(128, 16, 128),
        bf(128, 16, 128),
        bf(128, 16, 128),
        bf(128, 16, 128),
        bf(640, 2048),
        fl(512, 128),
        fl(128, 8, 128),
        fl(8, 128),
        fl(512, 128),
        fl(128, 8, 128),
        fl(8, 128),
        pltpu.SemaphoreType.DMA((6,)),
        pltpu.SemaphoreType.DMA((2,)),
        pltpu.SemaphoreType.DMA((12,)),
        pltpu.SemaphoreType.DMA((12,)),
    ]
    shapes = [
        jax.ShapeDtypeStruct((CELLS, CH), BF16),
        jax.ShapeDtypeStruct((CELLS, CH), BF16),
        jax.ShapeDtypeStruct((1, CH), F32),
        jax.ShapeDtypeStruct((CH, 640), F32),
        jax.ShapeDtypeStruct((1, CH), F32),
        jax.ShapeDtypeStruct((CH, CH), F32),
    ]
    params = (in_gain.reshape(1, CH), w_in, out_gain.reshape(1, CH), w_out)
    sums_shape = jax.ShapeDtypeStruct((512, 128), F32)
    results = pl.pallas_call(
        kernel,
        out_shape=shapes[:2] + [sums_shape] * 2,
        in_specs=[hbm] * 6,
        out_specs=[hbm] * 4,
        scratch_shapes=scratch,
        compiler_params=pltpu.CompilerParams(
            collective_id=0, has_side_effects=True, vmem_limit_bytes=VMEM_BYTES
        ),
        name="triangle_update",
    )(pair.reshape(CELLS, CH), cotangent.reshape(CELLS, CH), *params)
    pair_next, pair_back, in_gain_grad, w_in_grad, out_gain_grad, w_out_grad = pl.pallas_call(
        deliver,
        out_shape=shapes,
        in_specs=[hbm] * 8,
        out_specs=[hbm] * 6,
        scratch_shapes=[
            bf(CELLS, CH),
            bf(CELLS, CH),
            fl(512, 128),
            fl(512, 128),
            fl(1, CH),
            bf(CH, 640),
            fl(1, CH),
            bf(CH, CH),
            fl(1, CH),
            fl(CH, 640),
            fl(1, CH),
            fl(CH, CH),
            pltpu.SemaphoreType.DMA((8,)),
            pltpu.SemaphoreType.DMA((6,)),
        ],
        compiler_params=pltpu.CompilerParams(vmem_limit_bytes=VMEM_BYTES),
        name="deliver",
    )(*results, *params)
    return (
        pair_next.reshape(64, 32, CH),
        pair_back.reshape(64, 32, CH),
        in_gain_grad.reshape(CH),
        w_in_grad,
        out_gain_grad.reshape(CH),
        w_out_grad,
    )


def solution(mesh):
    in_specs = (P("row", "col", None), P("row", "col", None), P(), P(), P(), P())
    out_specs = (P("row", "col", None), P("row", "col", None), P(), P(), P(), P())
    return jax.shard_map(
        on_device, mesh=mesh, in_specs=in_specs, out_specs=out_specs, check_vma=False
    )
```

```python
import itertools

import jax
import jax.numpy as jnp
from jax import lax
from jax.experimental import pallas as pl
from jax.experimental.pallas import tpu as pltpu
from jax.sharding import PartitionSpec as P

EPSILON = 1e-05
LOGICAL = pl.DeviceIdType.LOGICAL
DEVICES = 128
CHIPS = 64
CH = 128
CELLS = 2048
CHUNK = 256
TILES = CHUNK // 128
STEPS = CELLS // CHUNK
VMEM_BYTES = 63 * 2**20
F32 = jnp.float32
BF16 = jnp.bfloat16
HOPS = sorted(itertools.product((0, 1, 2), repeat=3), key=lambda hops: (-sum(hops), hops))[:-1]


def matmul(a, b):
    return jnp.dot(a, b, preferred_element_type=F32)


def matmul_nt(a, b):
    return lax.dot_general(a, b, (((1,), (1,)), ((), ())), preferred_element_type=F32)


def parts():
    row, col = lax.axis_index("row"), lax.axis_index("col")
    x, y, z, core = (row // 4) * 2 + col // 8, (col // 2) % 4, row % 4, col % 2
    xs = [((x + d) % 4 // 2) * 64 + ((x + d) % 4 % 2) * 8 for d in range(4)]
    ys = [((y + d) % 4) * 2 for d in range(4)]
    zs = [((z + d) % 4) * 16 for d in range(4)]
    return xs, ys, zs, core


def for_chips(place, act):
    for hops in HOPS:
        ways = [(1, 3) if h == 1 else (h,) for h in hops]
        for dx, dy, dz in itertools.product(*ways):
            act(place[0][dx] + place[1][dy] + place[2][dz])


def greet(place, sibling):
    barrier = pltpu.get_barrier_semaphore()

    def signal(device):
        pl.semaphore_signal(barrier, inc=1, device_id=device, device_id_type=LOGICAL)

    def act(device):
        signal(device)
        signal(device + 1)

    for_chips(place, act)
    signal(sibling)


def remote(src, dst, send, recv, device):
    return pltpu.make_async_remote_copy(
        src_ref=src, dst_ref=dst, send_sem=send, recv_sem=recv, device_id=device, device_id_type=LOGICAL
    )


def send_to(core, place, src, dst, send, recv, me):
    def act(device):
        remote(src.at[device + core], dst.at[me], send, recv, device + core).start()

    for_chips(place, act)


def send_near(sibling, src, dst, send, recv, me):
    remote(src.at[sibling], dst.at[me], send, recv, sibling).start()
    pltpu.make_async_copy(src.at[me], dst.at[me], recv).start()


def wait_all(ref, sem):
    pltpu.make_async_copy(ref, ref, sem).wait()


def wait_sent(ref, sem):
    part = ref.at[pl.ds(0, ref.shape[0] - 1)]
    pltpu.make_async_copy(part, part, sem).wait()


def block(index):
    return pl.ds(index * 128, 128)


def cells_of(chunk):
    return pl.ds(pl.multiple_of(chunk * CHUNK, CHUNK), CHUNK)


def gather_matrix(received, perm, whole):
    rows = [
        jnp.concatenate([received[:, q_hi * 4 + q_lo].reshape(128, 128) for q_lo in range(4)], axis=1)
        for q_hi in range(4)
    ]
    moved = matmul(jnp.concatenate(rows, axis=0), perm[...]).astype(BF16)
    for q_hi in range(4):
        for i_lo in range(4):
            whole[block(i_lo), block(q_hi)] = tile(moved, q_hi, i_lo)


def scatter_matrix(whole, perm, outgoing):
    whole = whole.astype(BF16)
    rows = [
        jnp.concatenate([tile(whole, i_lo, q_hi) for i_lo in range(4)], axis=1) for q_hi in range(4)
    ]
    moved = matmul(jnp.concatenate(rows, axis=0), perm[...]).astype(BF16)
    for q_hi in range(4):
        for q_lo in range(4):
            outgoing[:, q_hi * 4 + q_lo] = tile(moved, q_hi, q_lo).reshape(8, 16, 128)


def tile(value, i, j):
    return value[i * 128 : (i + 1) * 128, j * 128 : (j + 1) * 128]


def put_tiles(spread, base, chunk, value):
    for t in range(TILES):
        spread[pl.ds(base + chunk * TILES + t, 128, stride=16), :] = value[:, t * 128 : (t + 1) * 128]


def get_tiles(spread, base, chunk):
    tiles = [spread[pl.ds(base + chunk * TILES + t, 128, stride=16), :] for t in range(TILES)]
    return jnp.concatenate(tiles, axis=1)


def put_row(rows, index, value):
    rows[pl.ds(index, 128, stride=4), :] = value


def get_row(rows, index):
    return rows[pl.ds(index, 128, stride=4), :]


def sums_scatter(place, send, recv, sums, received, total, totals, first, chip, core):
    tiles = sums.reshape(CHIPS, 8, 128)

    def act(device):
        remote(
            tiles.at[device // 2], received.at[chip], send.at[first], recv.at[first], device + core
        ).start()

    for_chips(place, act)
    pltpu.make_async_copy(tiles.at[chip], received.at[chip], recv.at[first]).start()


def sums_add(sibling, send, recv, sums, received, total, totals, first, chip, core):
    wait_all(received, recv.at[first])
    total[0] = jnp.sum(received[...], axis=0) * (1.0 / 512.0)
    swap = remote(total.at[0], total.at[1], send.at[first + 1], recv.at[first + 1], sibling)
    swap.start()
    swap.wait()
    total[2] = total[0] + total[1]


def sums_gather(place, send, recv, sums, received, total, totals, first, chip, core):
    whole = totals.reshape(CHIPS, 8, 128)

    def act(device):
        remote(total.at[2], whole.at[chip], send.at[first + 2], recv.at[first + 2], device + core).start()

    for_chips(place, act)
    pltpu.make_async_copy(total.at[2], whole.at[chip], recv.at[first + 2]).start()


def kernel(
    pair_hbm,
    cot_hbm,
    in_gain_hbm,
    w_in_hbm,
    out_gain_hbm,
    w_out_hbm,
    next_hbm,
    back_hbm,
    early_totals,
    late_totals,
    next_ref,
    back_ref,
    pair_ref,
    cot_ref,
    in_gain_ref,
    w_in_ref,
    out_gain_ref,
    w_out_ref,
    w_in_t,
    w_out_t,
    in_gain_t,
    out_gain_t,
    perm,
    rows_perm,
    rows_perm_t,
    pair_t,
    cot_t,
    hat,
    rstd,
    normed,
    left_a,
    left_b,
    right_a,
    right_b,
    gate,
    proj_cot,
    scaled,
    tri_hat,
    tri_normed,
    spread,
    l_out,
    l_in,
    r_out,
    r_in,
    left,
    right_raw,
    right,
    tri_out,
    tri_in,
    tc_out,
    tc_in,
    tc,
    tc_t,
    lc_out,
    lc_in,
    rc_out,
    rc_in,
    project_cot,
    early_sums,
    early_in,
    early_total,
    late_sums,
    late_in,
    late_total,
    load,
    store,
    send,
    recv,
):
    *place, core = parts()
    me = lax.axis_index("row") * 16 + lax.axis_index("col")
    chip = me // 2
    sibling = me + 1 - 2 * core
    loads = [
        pltpu.make_async_copy(src, dst, load.at[n])
        for n, (src, dst) in enumerate(
            (
                (pair_hbm, pair_ref),
                (w_in_hbm, w_in_ref),
                (in_gain_hbm, in_gain_ref),
                (cot_hbm, cot_ref),
                (w_out_hbm, w_out_ref),
                (out_gain_hbm, out_gain_ref),
            )
        )
    ]
    for copy in loads:
        copy.start()
    greet(place, sibling)

    for copy in loads[:3]:
        copy.wait()
    for n in range(5):
        w_in_t[block(n), :] = w_in_ref[:, block(n)].T
    in_gain_t[...] = jnp.broadcast_to(in_gain_ref[...], (128, 128)).T

    def project(chunk, carry):
        cells = cells_of(chunk)
        x = pair_ref[cells, :].astype(F32).T
        pair_t[:, cells] = x
        center = x - jnp.mean(x, axis=0, keepdims=True)
        inverse = lax.rsqrt(jnp.mean(center * center, axis=0, keepdims=True) + EPSILON)
        x_hat = center * inverse
        hat[:, cells] = x_hat
        rstd[:, cells] = inverse
        y = (x_hat * in_gain_t[:, :1]).astype(BF16)
        normed[:, cells] = y
        for side, (keep_a, keep_b) in enumerate(((left_a, left_b), (right_a, right_b))):
            both = matmul(w_in_t[pl.ds(side * 256, 256), :], y)
            sig = jax.nn.sigmoid(both[:128])
            act = sig * both[128:]
            keep_b[:, cells] = sig
            keep_a[:, cells] = act * (1.0 - sig)
            put_tiles(spread, side * 2048, chunk, act)
        return carry

    lax.fori_loop(0, STEPS, project, 0, unroll=4)
    r_out[...] = spread[pl.ds(2048, 2048), :].astype(BF16).reshape(128, 16, 128)
    pl.semaphore_wait(pltpu.get_barrier_semaphore(), DEVICES - 1)
    right_way = (r_out, r_in, send.at[0], recv.at[0], me)
    left_way = (l_out, l_in, send.at[1], recv.at[1], me)
    send_to(0, place, *right_way)
    l_out[...] = spread[pl.ds(0, 2048), :].astype(BF16).reshape(128, 16, 128)
    send_to(0, place, *left_way)
    send_to(1, place, *right_way)
    send_near(sibling, *right_way)
    send_to(1, place, *left_way)
    send_near(sibling, *left_way)

    a = lax.broadcasted_iota(jnp.int32, (512, 512), 0)
    b = lax.broadcasted_iota(jnp.int32, (512, 512), 1)
    swapped = ((a // 32) % 4) * 128 + (a // 128) * 32 + a % 32
    perm[...] = jnp.where(swapped == b, 1.0, 0.0).astype(BF16)
    rows_perm[...] = jnp.where((a % 4) * 128 + a // 4 == b, 1.0, 0.0).astype(BF16)
    rows_perm_t[...] = jnp.where((b % 4) * 128 + b // 4 == a, 1.0, 0.0).astype(BF16)
    for copy in loads[3:]:
        copy.wait()
    w_out_t[...] = w_out_ref[...].T
    out_gain_t[...] = jnp.broadcast_to(out_gain_ref[...], (128, 128)).T

    def upstream(chunk, carry):
        cells = cells_of(chunk)
        sig = jax.nn.sigmoid(matmul(w_in_t[pl.ds(512, 128), :], normed[:, cells]))
        gate[:, cells] = sig
        up = cot_ref[cells, :].astype(F32).T
        cot_t[:, cells] = up
        back = (up * sig).astype(BF16)
        proj_cot[:, cells] = back
        scaled[:, cells] = matmul(w_out_ref[...], back) * out_gain_t[:, :1]
        return carry

    lax.fori_loop(0, STEPS, upstream, 0)

    wait_all(r_in, recv.at[0])
    gather_matrix(r_in.reshape(8, 16, 16, 128), perm, right_raw)
    right[...] = matmul(rows_perm[...], right_raw[...]).astype(BF16)
    wait_all(l_in, recv.at[1])
    gather_matrix(l_in.reshape(8, 16, 16, 128), perm, left)
    scatter_matrix(matmul_nt(left[...], right[...]), perm, tri_out.reshape(8, 16, 16, 128))
    way = (tri_out, tri_in, send.at[2], recv.at[2], me)
    send_to(0, place, *way)
    send_to(1, place, *way)
    send_near(sibling, *way)
    wait_all(tri_in, recv.at[2])

    spread[pl.ds(0, 2048), :] = tri_in[...].reshape(2048, 128).astype(F32)

    def middle(chunk, carry):
        cells = cells_of(chunk)
        x = get_tiles(spread, 0, chunk)
        center = x - jnp.mean(x, axis=0, keepdims=True)
        inverse = lax.rsqrt(jnp.mean(center * center, axis=0, keepdims=True) + EPSILON)
        x_hat = center * inverse
        tri_hat[:, cells] = x_hat
        grad = scaled[:, cells]
        mean = jnp.mean(grad, axis=0, keepdims=True)
        along = jnp.mean(grad * x_hat, axis=0, keepdims=True)
        put_tiles(spread, 2048, chunk, inverse * (grad - mean - x_hat * along))
        return carry

    lax.fori_loop(0, STEPS, middle, 0, unroll=True)
    tc_out[...] = spread[pl.ds(2048, 2048), :].astype(BF16).reshape(128, 16, 128)
    way = (tc_out, tc_in, send.at[3], recv.at[3], me)
    send_to(0, place, *way)
    send_to(1, place, *way)
    send_near(sibling, *way)

    def update(chunk, carry):
        cells = cells_of(chunk)
        y = (tri_hat[:, cells] * out_gain_t[:, :1]).astype(BF16)
        tri_normed[:, cells] = y
        projected = matmul(w_out_t[...], y)
        sig = gate[:, cells]
        next_ref[cells, :] = (pair_t[:, cells] + sig * projected).T.astype(BF16)
        project_cot[pl.ds(512, 128), cells] = (
            cot_t[:, cells] * projected * sig * (1.0 - sig)
        ).astype(BF16)
        return carry

    lax.fori_loop(0, STEPS, update, 0)

    early = (early_sums, early_in, early_total, early_totals, 6, chip, core)
    late = (late_sums, late_in, late_total, late_totals, 9, chip, core)
    w_out_sum = matmul_nt(tri_normed[...], proj_cot[...])
    put_row(early_sums, 0, matmul_nt(normed[...], project_cot[block(4), :]))
    for n in (1, 2, 3):
        put_row(early_sums, n, w_out_sum)
    sums_scatter(place, send, recv, *early)
    next_copy = pltpu.make_async_copy(next_ref, next_hbm, store.at[0])
    next_copy.start()
    wait_all(tc_in, recv.at[3])

    gather_matrix(tc_in.reshape(8, 16, 16, 128), perm, tc)
    scatter_matrix(matmul(tc[...], right[...]), perm, lc_out.reshape(8, 16, 16, 128))
    left_way = (lc_out, lc_in, send.at[4], recv.at[4], me)
    send_to(0, place, *left_way)
    tc_t[...] = matmul_nt(rows_perm_t[...], tc[...]).astype(BF16)
    scatter_matrix(matmul(tc_t[...], left[...]), perm, rc_out.reshape(8, 16, 16, 128))
    right_way = (rc_out, rc_in, send.at[5], recv.at[5], me)
    send_to(0, place, *right_way)
    send_to(1, place, *left_way)
    send_near(sibling, *left_way)
    send_to(1, place, *right_way)
    send_near(sibling, *right_way)

    sums_add(sibling, send, recv, *early)

    for side, (got, keep_a, keep_b) in enumerate(((lc_in, left_a, left_b), (rc_in, right_a, right_b))):
        wait_all(got, recv.at[4 + side])
        spread[pl.ds(side * 2048, 2048), :] = got[...].reshape(2048, 128).astype(F32)

        def products(chunk, carry):
            cells = cells_of(chunk)
            grad = get_tiles(spread, side * 2048, chunk)
            project_cot[pl.ds(side * 256, 128), cells] = (grad * keep_a[:, cells]).astype(BF16)
            project_cot[pl.ds(side * 256 + 128, 128), cells] = (grad * keep_b[:, cells]).astype(BF16)
            return carry

        lax.fori_loop(0, STEPS, products, 0, unroll=True)
        part = matmul_nt(normed[...], project_cot[pl.ds(side * 256, 256), :])
        put_row(late_sums, 2 * side, part[:, :128])
        put_row(late_sums, 2 * side + 1, part[:, 128:])

    sums_scatter(place, send, recv, *late)
    sums_gather(place, send, recv, *early)

    def finish(chunk, carry):
        cells = cells_of(chunk)
        grad = matmul(w_in_ref[...], project_cot[:, cells]) * in_gain_t[:, :1]
        x_hat = hat[:, cells]
        mean = jnp.mean(grad, axis=0, keepdims=True)
        along = jnp.mean(grad * x_hat, axis=0, keepdims=True)
        back = rstd[:, cells] * (grad - mean - x_hat * along)
        back_ref[cells, :] = (cot_t[:, cells] + back).T.astype(BF16)
        return carry

    lax.fori_loop(0, STEPS, finish, 0, unroll=2)
    back_copy = pltpu.make_async_copy(back_ref, back_hbm, store.at[1])
    back_copy.start()
    sums_add(sibling, send, recv, *late)
    sums_gather(place, send, recv, *late)
    wait_all(early_totals, recv.at[8])
    wait_all(late_totals, recv.at[11])

    next_copy.wait()
    back_copy.wait()
    wait_sent(r_out, send.at[0])
    wait_sent(l_out, send.at[1])
    wait_sent(tri_out, send.at[2])
    wait_sent(tc_out, send.at[3])
    wait_sent(lc_out, send.at[4])
    wait_sent(rc_out, send.at[5])
    for n in (6, 8, 9, 11):
        wait_sent(early_in, send.at[n])


def deliver(
    next_hbm,
    back_hbm,
    early_hbm,
    late_hbm,
    in_gain_hbm,
    w_in_hbm,
    out_gain_hbm,
    w_out_hbm,
    next_out,
    back_out,
    in_gain_grad_out,
    w_in_grad_out,
    out_gain_grad_out,
    w_out_grad_out,
    next_ref,
    back_ref,
    early,
    late,
    in_gain,
    w_in,
    out_gain,
    w_out,
    in_gain_grad,
    w_in_grad,
    out_gain_grad,
    w_out_grad,
    load,
    store,
):
    sources = (early_hbm, late_hbm, in_gain_hbm, w_in_hbm, out_gain_hbm, w_out_hbm, next_hbm, back_hbm)
    holds = (early, late, in_gain, w_in, out_gain, w_out, next_ref, back_ref)
    loads = [pltpu.make_async_copy(src, dst, load.at[n]) for n, (src, dst) in enumerate(zip(sources, holds))]
    results = (next_ref, back_ref, in_gain_grad, w_in_grad, out_gain_grad, w_out_grad)
    places = (next_out, back_out, in_gain_grad_out, w_in_grad_out, out_gain_grad_out, w_out_grad_out)
    stores = [pltpu.make_async_copy(src, dst, store.at[n]) for n, (src, dst) in enumerate(zip(results, places))]
    for copy in loads:
        copy.start()
    for n in (0, 1):
        loads[6 + n].wait()
        stores[n].start()
    for copy in loads[:6]:
        copy.wait()
    along = jnp.zeros((128, 128), F32)
    for n in range(5):
        part = get_row(early, 0) if n == 4 else get_row(late, n)
        w_in_grad[:, block(n)] = part
        along += part * w_in[:, block(n)].astype(F32)
    stores[3].start()
    part = get_row(early, 1)
    w_out_grad[...] = part
    stores[5].start()
    in_gain_grad[...] = jnp.sum(along.T, axis=0, keepdims=True) / in_gain[...]
    along = part * w_out[...].astype(F32)
    out_gain_grad[...] = jnp.sum(along.T, axis=0, keepdims=True) / out_gain[...]
    stores[2].start()
    stores[4].start()
    for copy in stores:
        copy.wait()


def on_device(pair, cotangent, in_gain, w_in, out_gain, w_out):
    hbm = pl.BlockSpec(memory_space=pltpu.HBM)

    def bf(*shape):
        return pltpu.VMEM(shape, BF16)

    def fl(*shape):
        return pltpu.VMEM(shape, F32)

    scratch = [
        bf(2048, 128),
        bf(2048, 128),
        bf(2048, 128),
        bf(2048, 128),
        fl(1, 128),
        bf(128, 640),
        fl(1, 128),
        bf(128, 128),
        bf(640, 128),
        bf(128, 128),
        fl(128, 128),
        fl(128, 128),
        bf(512, 512),
        bf(512, 512),
        bf(512, 512),
        fl(128, 2048),
        fl(128, 2048),
        fl(128, 2048),
        fl(1, 2048),
        bf(128, 2048),
        fl(128, 2048),
        fl(128, 2048),
        fl(128, 2048),
        fl(128, 2048),
        fl(128, 2048),
        bf(128, 2048),
        fl(128, 2048),
        fl(128, 2048),
        bf(128, 2048),
        fl(4096, 128),
        bf(128, 16, 128),
        bf(128, 16, 128),
        bf(128, 16, 128),
        bf(128, 16, 128),
        bf(512, 512),
        bf(512, 512),
        bf(512, 512),
        bf(128, 16, 128),
        bf(128, 16, 128),
        bf(128, 16, 128),
        bf(128, 16, 128),
        bf(512, 512),
        bf(512, 512),
        bf(128, 16, 128),
        bf(128, 16, 128),
        bf(128, 16, 128),
        bf(128, 16, 128),
        bf(640, 2048),
        fl(512, 128),
        fl(64, 8, 128),
        fl(3, 8, 128),
        fl(512, 128),
        fl(64, 8, 128),
        fl(3, 8, 128),
        pltpu.SemaphoreType.DMA((6,)),
        pltpu.SemaphoreType.DMA((2,)),
        pltpu.SemaphoreType.DMA((12,)),
        pltpu.SemaphoreType.DMA((12,)),
    ]
    shapes = [
        jax.ShapeDtypeStruct((CELLS, CH), BF16),
        jax.ShapeDtypeStruct((CELLS, CH), BF16),
        jax.ShapeDtypeStruct((1, CH), F32),
        jax.ShapeDtypeStruct((CH, 640), F32),
        jax.ShapeDtypeStruct((1, CH), F32),
        jax.ShapeDtypeStruct((CH, CH), F32),
    ]
    params = (in_gain.reshape(1, CH), w_in, out_gain.reshape(1, CH), w_out)
    sums_shape = jax.ShapeDtypeStruct((512, 128), F32)
    results = pl.pallas_call(
        kernel,
        out_shape=shapes[:2] + [sums_shape] * 2,
        in_specs=[hbm] * 6,
        out_specs=[hbm] * 4,
        scratch_shapes=scratch,
        compiler_params=pltpu.CompilerParams(
            collective_id=0, has_side_effects=True, vmem_limit_bytes=VMEM_BYTES
        ),
        name="triangle_update",
    )(pair.reshape(CELLS, CH), cotangent.reshape(CELLS, CH), *params)
    pair_next, pair_back, in_gain_grad, w_in_grad, out_gain_grad, w_out_grad = pl.pallas_call(
        deliver,
        out_shape=shapes,
        in_specs=[hbm] * 8,
        out_specs=[hbm] * 6,
        scratch_shapes=[
            bf(CELLS, CH),
            bf(CELLS, CH),
            fl(512, 128),
            fl(512, 128),
            fl(1, CH),
            bf(CH, 640),
            fl(1, CH),
            bf(CH, CH),
            fl(1, CH),
            fl(CH, 640),
            fl(1, CH),
            fl(CH, CH),
            pltpu.SemaphoreType.DMA((8,)),
            pltpu.SemaphoreType.DMA((6,)),
        ],
        compiler_params=pltpu.CompilerParams(vmem_limit_bytes=VMEM_BYTES),
        name="deliver",
    )(*results, *params)
    return (
        pair_next.reshape(64, 32, CH),
        pair_back.reshape(64, 32, CH),
        in_gain_grad.reshape(CH),
        w_in_grad,
        out_gain_grad.reshape(CH),
        w_out_grad,
    )


def solution(mesh):
    in_specs = (P("row", "col", None), P("row", "col", None), P(), P(), P(), P())
    out_specs = (P("row", "col", None), P("row", "col", None), P(), P(), P(), P())
    return jax.shard_map(
        on_device, mesh=mesh, in_specs=in_specs, out_specs=out_specs, check_vma=False
    )
```

```python
import itertools

import jax
import jax.numpy as jnp
from jax import lax
from jax.experimental import pallas as pl
from jax.experimental.pallas import tpu as pltpu
from jax.sharding import PartitionSpec as P

EPSILON = 1e-05
LOGICAL = pl.DeviceIdType.LOGICAL
DEVICES = 128
CHIPS = 64
CH = 128
CELLS = 2048
CHUNK = 256
TILES = CHUNK // 128
STEPS = CELLS // CHUNK
VMEM_BYTES = 63 * 2**20
F32 = jnp.float32
BF16 = jnp.bfloat16
HOPS = sorted(itertools.product((0, 1, 2), repeat=3), key=lambda hops: (-sum(hops), hops))[:-1]


def matmul(a, b):
    return jnp.dot(a, b, preferred_element_type=F32)


def matmul_nt(a, b):
    return lax.dot_general(a, b, (((1,), (1,)), ((), ())), preferred_element_type=F32)


def parts():
    row, col = lax.axis_index("row"), lax.axis_index("col")
    x, y, z, core = (row // 4) * 2 + col // 8, (col // 2) % 4, row % 4, col % 2
    xs = [((x + d) % 4 // 2) * 64 + ((x + d) % 4 % 2) * 8 for d in range(4)]
    ys = [((y + d) % 4) * 2 for d in range(4)]
    zs = [((z + d) % 4) * 16 for d in range(4)]
    return xs, ys, zs, core


def for_chips(place, act):
    for hops in HOPS:
        ways = [(1, 3) if h == 1 else (h,) for h in hops]
        for dx, dy, dz in itertools.product(*ways):
            act(place[0][dx] + place[1][dy] + place[2][dz])


def greet(place, sibling):
    barrier = pltpu.get_barrier_semaphore()

    def signal(device):
        pl.semaphore_signal(barrier, inc=1, device_id=device, device_id_type=LOGICAL)

    def act(device):
        signal(device)
        signal(device + 1)

    for_chips(place, act)
    signal(sibling)


def remote(src, dst, send, recv, device):
    return pltpu.make_async_remote_copy(
        src_ref=src, dst_ref=dst, send_sem=send, recv_sem=recv, device_id=device, device_id_type=LOGICAL
    )


def send_to(core, place, src, dst, send, recv, me):
    def act(device):
        remote(src.at[device + core], dst.at[me], send, recv, device + core).start()

    for_chips(place, act)


def send_near(sibling, src, dst, send, recv, me):
    remote(src.at[sibling], dst.at[me], send, recv, sibling).start()
    pltpu.make_async_copy(src.at[me], dst.at[me], recv).start()


def wait_all(ref, sem):
    pltpu.make_async_copy(ref, ref, sem).wait()


def wait_sent(ref, sem):
    part = ref.at[pl.ds(0, ref.shape[0] - 1)]
    pltpu.make_async_copy(part, part, sem).wait()


def block(index):
    return pl.ds(index * 128, 128)


def cells_of(chunk):
    return pl.ds(pl.multiple_of(chunk * CHUNK, CHUNK), CHUNK)


def gather_matrix(received, perm, whole):
    rows = [
        jnp.concatenate([received[:, q_hi * 4 + q_lo].reshape(128, 128) for q_lo in range(4)], axis=1)
        for q_hi in range(4)
    ]
    moved = matmul(jnp.concatenate(rows, axis=0), perm[...]).astype(BF16)
    for q_hi in range(4):
        for i_lo in range(4):
            whole[block(i_lo), block(q_hi)] = tile(moved, q_hi, i_lo)


def scatter_matrix(whole, perm, outgoing):
    whole = whole.astype(BF16)
    rows = [
        jnp.concatenate([tile(whole, i_lo, q_hi) for i_lo in range(4)], axis=1) for q_hi in range(4)
    ]
    moved = matmul(jnp.concatenate(rows, axis=0), perm[...]).astype(BF16)
    for q_hi in range(4):
        for q_lo in range(4):
            outgoing[:, q_hi * 4 + q_lo] = tile(moved, q_hi, q_lo).reshape(8, 16, 128)


def tile(value, i, j):
    return value[i * 128 : (i + 1) * 128, j * 128 : (j + 1) * 128]


def put_tiles(spread, base, chunk, value):
    for t in range(TILES):
        spread[pl.ds(base + chunk * TILES + t, 128, stride=16), :] = value[:, t * 128 : (t + 1) * 128]


def get_tiles(spread, base, chunk):
    tiles = [spread[pl.ds(base + chunk * TILES + t, 128, stride=16), :] for t in range(TILES)]
    return jnp.concatenate(tiles, axis=1)


def put_row(rows, index, value):
    rows[pl.ds(index, 128, stride=4), :] = value


def get_row(rows, index):
    return rows[pl.ds(index, 128, stride=4), :]


def sums_scatter(place, send, recv, sums, received, total, totals, first, chip, core):
    tiles = sums.reshape(CHIPS, 8, 128)

    def act(device):
        remote(
            tiles.at[device // 2], received.at[chip], send.at[first], recv.at[first], device + core
        ).start()

    for_chips(place, act)
    pltpu.make_async_copy(tiles.at[chip], received.at[chip], recv.at[first]).start()


def sums_add(sibling, send, recv, sums, received, total, totals, first, chip, core):
    wait_all(received, recv.at[first])
    total[0] = jnp.sum(received[...], axis=0) * (1.0 / 512.0)
    swap = remote(total.at[0], total.at[1], send.at[first + 1], recv.at[first + 1], sibling)
    swap.start()
    swap.wait()
    total[2] = total[0] + total[1]


def sums_gather(place, send, recv, sums, received, total, totals, first, chip, core):
    whole = totals.reshape(CHIPS, 8, 128)

    def act(device):
        remote(total.at[2], whole.at[chip], send.at[first + 2], recv.at[first + 2], device + core).start()

    for_chips(place, act)
    pltpu.make_async_copy(total.at[2], whole.at[chip], recv.at[first + 2]).start()


def kernel(
    pair_hbm,
    cot_hbm,
    in_gain_hbm,
    w_in_hbm,
    out_gain_hbm,
    w_out_hbm,
    next_hbm,
    back_hbm,
    early_totals,
    late_totals,
    next_ref,
    back_ref,
    pair_ref,
    cot_ref,
    in_gain_ref,
    w_in_ref,
    out_gain_ref,
    w_out_ref,
    w_in_t,
    w_out_t,
    in_gain_t,
    out_gain_t,
    perm,
    rows_perm,
    rows_perm_t,
    pair_t,
    cot_t,
    hat,
    rstd,
    normed,
    left_a,
    left_b,
    right_a,
    right_b,
    gate,
    proj_cot,
    scaled,
    tri_hat,
    tri_normed,
    spread,
    l_out,
    l_in,
    r_out,
    r_in,
    left,
    right_raw,
    right,
    tri_out,
    tri_in,
    tc_out,
    tc_in,
    tc,
    tc_t,
    lc_out,
    lc_in,
    rc_out,
    rc_in,
    project_cot,
    early_sums,
    early_in,
    early_total,
    late_sums,
    late_in,
    late_total,
    load,
    store,
    send,
    recv,
):
    *place, core = parts()
    me = lax.axis_index("row") * 16 + lax.axis_index("col")
    chip = me // 2
    sibling = me + 1 - 2 * core
    loads = [
        pltpu.make_async_copy(src, dst, load.at[n])
        for n, (src, dst) in enumerate(
            (
                (pair_hbm, pair_ref),
                (w_in_hbm, w_in_ref),
                (in_gain_hbm, in_gain_ref),
                (cot_hbm, cot_ref),
                (w_out_hbm, w_out_ref),
                (out_gain_hbm, out_gain_ref),
            )
        )
    ]
    for copy in loads:
        copy.start()
    greet(place, sibling)

    a = lax.broadcasted_iota(jnp.int32, (512, 512), 0)
    b = lax.broadcasted_iota(jnp.int32, (512, 512), 1)
    swapped = ((a // 32) % 4) * 128 + (a // 128) * 32 + a % 32
    perm[...] = jnp.where(swapped == b, 1.0, 0.0).astype(BF16)
    rows_perm[...] = jnp.where((a % 4) * 128 + a // 4 == b, 1.0, 0.0).astype(BF16)
    rows_perm_t[...] = jnp.where((b % 4) * 128 + b // 4 == a, 1.0, 0.0).astype(BF16)
    for copy in loads:
        copy.wait()
    for n in range(5):
        w_in_t[block(n), :] = w_in_ref[:, block(n)].T
    w_out_t[...] = w_out_ref[...].T
    in_gain_t[...] = jnp.broadcast_to(in_gain_ref[...], (128, 128)).T
    out_gain_t[...] = jnp.broadcast_to(out_gain_ref[...], (128, 128)).T

    def project(chunk, carry):
        cells = cells_of(chunk)
        x = pair_ref[cells, :].astype(F32).T
        pair_t[:, cells] = x
        center = x - jnp.mean(x, axis=0, keepdims=True)
        inverse = lax.rsqrt(jnp.mean(center * center, axis=0, keepdims=True) + EPSILON)
        x_hat = center * inverse
        hat[:, cells] = x_hat
        rstd[:, cells] = inverse
        y = (x_hat * in_gain_t[:, :1]).astype(BF16)
        normed[:, cells] = y
        for side, (keep_a, keep_b) in enumerate(((left_a, left_b), (right_a, right_b))):
            both = matmul(w_in_t[pl.ds(side * 256, 256), :], y)
            sig = jax.nn.sigmoid(both[:128])
            act = sig * both[128:]
            keep_b[:, cells] = sig
            keep_a[:, cells] = act * (1.0 - sig)
            put_tiles(spread, side * 2048, chunk, act)
        return carry

    lax.fori_loop(0, STEPS, project, 0, unroll=4)
    r_out[...] = spread[pl.ds(2048, 2048), :].astype(BF16).reshape(128, 16, 128)
    pl.semaphore_wait(pltpu.get_barrier_semaphore(), DEVICES - 1)
    right_way = (r_out, r_in, send.at[0], recv.at[0], me)
    left_way = (l_out, l_in, send.at[1], recv.at[1], me)
    send_to(0, place, *right_way)
    l_out[...] = spread[pl.ds(0, 2048), :].astype(BF16).reshape(128, 16, 128)
    send_to(0, place, *left_way)
    send_to(1, place, *right_way)
    send_near(sibling, *right_way)
    send_to(1, place, *left_way)
    send_near(sibling, *left_way)

    def upstream(chunk, carry):
        cells = cells_of(chunk)
        sig = jax.nn.sigmoid(matmul(w_in_t[pl.ds(512, 128), :], normed[:, cells]))
        gate[:, cells] = sig
        up = cot_ref[cells, :].astype(F32).T
        cot_t[:, cells] = up
        back = (up * sig).astype(BF16)
        proj_cot[:, cells] = back
        scaled[:, cells] = matmul(w_out_ref[...], back) * out_gain_t[:, :1]
        return carry

    lax.fori_loop(0, STEPS, upstream, 0)

    wait_all(r_in, recv.at[0])
    gather_matrix(r_in.reshape(8, 16, 16, 128), perm, right_raw)
    right[...] = matmul(rows_perm[...], right_raw[...]).astype(BF16)
    wait_all(l_in, recv.at[1])
    gather_matrix(l_in.reshape(8, 16, 16, 128), perm, left)
    scatter_matrix(matmul_nt(left[...], right[...]), perm, tri_out.reshape(8, 16, 16, 128))
    way = (tri_out, tri_in, send.at[2], recv.at[2], me)
    send_to(0, place, *way)
    send_to(1, place, *way)
    send_near(sibling, *way)
    wait_all(tri_in, recv.at[2])

    spread[pl.ds(0, 2048), :] = tri_in[...].reshape(2048, 128).astype(F32)

    def middle(chunk, carry):
        cells = cells_of(chunk)
        x = get_tiles(spread, 0, chunk)
        center = x - jnp.mean(x, axis=0, keepdims=True)
        inverse = lax.rsqrt(jnp.mean(center * center, axis=0, keepdims=True) + EPSILON)
        x_hat = center * inverse
        tri_hat[:, cells] = x_hat
        grad = scaled[:, cells]
        mean = jnp.mean(grad, axis=0, keepdims=True)
        along = jnp.mean(grad * x_hat, axis=0, keepdims=True)
        put_tiles(spread, 2048, chunk, inverse * (grad - mean - x_hat * along))
        return carry

    lax.fori_loop(0, STEPS, middle, 0, unroll=True)
    tc_out[...] = spread[pl.ds(2048, 2048), :].astype(BF16).reshape(128, 16, 128)
    way = (tc_out, tc_in, send.at[3], recv.at[3], me)
    send_to(0, place, *way)
    send_to(1, place, *way)
    send_near(sibling, *way)

    def update(chunk, carry):
        cells = cells_of(chunk)
        y = (tri_hat[:, cells] * out_gain_t[:, :1]).astype(BF16)
        tri_normed[:, cells] = y
        projected = matmul(w_out_t[...], y)
        sig = gate[:, cells]
        next_ref[cells, :] = (pair_t[:, cells] + sig * projected).T.astype(BF16)
        project_cot[pl.ds(512, 128), cells] = (
            cot_t[:, cells] * projected * sig * (1.0 - sig)
        ).astype(BF16)
        return carry

    lax.fori_loop(0, STEPS, update, 0)

    early = (early_sums, early_in, early_total, early_totals, 6, chip, core)
    late = (late_sums, late_in, late_total, late_totals, 9, chip, core)
    w_out_sum = matmul_nt(tri_normed[...], proj_cot[...])
    put_row(early_sums, 0, matmul_nt(normed[...], project_cot[block(4), :]))
    for n in (1, 2, 3):
        put_row(early_sums, n, w_out_sum)
    sums_scatter(place, send, recv, *early)
    next_copy = pltpu.make_async_copy(next_ref, next_hbm, store.at[0])
    next_copy.start()
    wait_all(tc_in, recv.at[3])

    gather_matrix(tc_in.reshape(8, 16, 16, 128), perm, tc)
    scatter_matrix(matmul(tc[...], right[...]), perm, lc_out.reshape(8, 16, 16, 128))
    left_way = (lc_out, lc_in, send.at[4], recv.at[4], me)
    send_to(0, place, *left_way)
    tc_t[...] = matmul_nt(rows_perm_t[...], tc[...]).astype(BF16)
    scatter_matrix(matmul(tc_t[...], left[...]), perm, rc_out.reshape(8, 16, 16, 128))
    right_way = (rc_out, rc_in, send.at[5], recv.at[5], me)
    send_to(0, place, *right_way)
    send_to(1, place, *left_way)
    send_near(sibling, *left_way)
    send_to(1, place, *right_way)
    send_near(sibling, *right_way)

    sums_add(sibling, send, recv, *early)

    for side, (got, keep_a, keep_b) in enumerate(((lc_in, left_a, left_b), (rc_in, right_a, right_b))):
        wait_all(got, recv.at[4 + side])
        spread[pl.ds(side * 2048, 2048), :] = got[...].reshape(2048, 128).astype(F32)

        def products(chunk, carry):
            cells = cells_of(chunk)
            grad = get_tiles(spread, side * 2048, chunk)
            project_cot[pl.ds(side * 256, 128), cells] = (grad * keep_a[:, cells]).astype(BF16)
            project_cot[pl.ds(side * 256 + 128, 128), cells] = (grad * keep_b[:, cells]).astype(BF16)
            return carry

        lax.fori_loop(0, STEPS, products, 0, unroll=True)
        part = matmul_nt(normed[...], project_cot[pl.ds(side * 256, 256), :])
        put_row(late_sums, 2 * side, part[:, :128])
        put_row(late_sums, 2 * side + 1, part[:, 128:])

    sums_scatter(place, send, recv, *late)

    def finish(chunk, carry):
        cells = cells_of(chunk)
        grad = matmul(w_in_ref[...], project_cot[:, cells]) * in_gain_t[:, :1]
        x_hat = hat[:, cells]
        mean = jnp.mean(grad, axis=0, keepdims=True)
        along = jnp.mean(grad * x_hat, axis=0, keepdims=True)
        back = rstd[:, cells] * (grad - mean - x_hat * along)
        back_ref[cells, :] = (cot_t[:, cells] + back).T.astype(BF16)
        return carry

    lax.fori_loop(0, STEPS, finish, 0, unroll=2)
    back_copy = pltpu.make_async_copy(back_ref, back_hbm, store.at[1])
    back_copy.start()
    sums_gather(place, send, recv, *early)
    sums_add(sibling, send, recv, *late)
    sums_gather(place, send, recv, *late)
    wait_all(early_totals, recv.at[8])
    wait_all(late_totals, recv.at[11])

    next_copy.wait()
    back_copy.wait()
    wait_sent(r_out, send.at[0])
    wait_sent(l_out, send.at[1])
    wait_sent(tri_out, send.at[2])
    wait_sent(tc_out, send.at[3])
    wait_sent(lc_out, send.at[4])
    wait_sent(rc_out, send.at[5])
    for n in (6, 8, 9, 11):
        wait_sent(early_in, send.at[n])


def deliver(
    next_hbm,
    back_hbm,
    early_hbm,
    late_hbm,
    in_gain_hbm,
    w_in_hbm,
    out_gain_hbm,
    w_out_hbm,
    next_out,
    back_out,
    in_gain_grad_out,
    w_in_grad_out,
    out_gain_grad_out,
    w_out_grad_out,
    next_ref,
    back_ref,
    early,
    late,
    in_gain,
    w_in,
    out_gain,
    w_out,
    in_gain_grad,
    w_in_grad,
    out_gain_grad,
    w_out_grad,
    load,
    store,
):
    sources = (early_hbm, late_hbm, in_gain_hbm, w_in_hbm, out_gain_hbm, w_out_hbm, next_hbm, back_hbm)
    holds = (early, late, in_gain, w_in, out_gain, w_out, next_ref, back_ref)
    loads = [pltpu.make_async_copy(src, dst, load.at[n]) for n, (src, dst) in enumerate(zip(sources, holds))]
    results = (next_ref, back_ref, in_gain_grad, w_in_grad, out_gain_grad, w_out_grad)
    places = (next_out, back_out, in_gain_grad_out, w_in_grad_out, out_gain_grad_out, w_out_grad_out)
    stores = [pltpu.make_async_copy(src, dst, store.at[n]) for n, (src, dst) in enumerate(zip(results, places))]
    for copy in loads:
        copy.start()
    for n in (0, 1):
        loads[6 + n].wait()
        stores[n].start()
    for copy in loads[:6]:
        copy.wait()
    along = jnp.zeros((128, 128), F32)
    for n in range(5):
        part = get_row(early, 0) if n == 4 else get_row(late, n)
        w_in_grad[:, block(n)] = part
        along += part * w_in[:, block(n)].astype(F32)
    stores[3].start()
    part = get_row(early, 1)
    w_out_grad[...] = part
    stores[5].start()
    in_gain_grad[...] = jnp.sum(along.T, axis=0, keepdims=True) / in_gain[...]
    along = part * w_out[...].astype(F32)
    out_gain_grad[...] = jnp.sum(along.T, axis=0, keepdims=True) / out_gain[...]
    stores[2].start()
    stores[4].start()
    for copy in stores:
        copy.wait()


def on_device(pair, cotangent, in_gain, w_in, out_gain, w_out):
    hbm = pl.BlockSpec(memory_space=pltpu.HBM)

    def bf(*shape):
        return pltpu.VMEM(shape, BF16)

    def fl(*shape):
        return pltpu.VMEM(shape, F32)

    scratch = [
        bf(2048, 128),
        bf(2048, 128),
        bf(2048, 128),
        bf(2048, 128),
        fl(1, 128),
        bf(128, 640),
        fl(1, 128),
        bf(128, 128),
        bf(640, 128),
        bf(128, 128),
        fl(128, 128),
        fl(128, 128),
        bf(512, 512),
        bf(512, 512),
        bf(512, 512),
        fl(128, 2048),
        fl(128, 2048),
        fl(128, 2048),
        fl(1, 2048),
        bf(128, 2048),
        fl(128, 2048),
        fl(128, 2048),
        fl(128, 2048),
        fl(128, 2048),
        fl(128, 2048),
        bf(128, 2048),
        fl(128, 2048),
        fl(128, 2048),
        bf(128, 2048),
        fl(4096, 128),
        bf(128, 16, 128),
        bf(128, 16, 128),
        bf(128, 16, 128),
        bf(128, 16, 128),
        bf(512, 512),
        bf(512, 512),
        bf(512, 512),
        bf(128, 16, 128),
        bf(128, 16, 128),
        bf(128, 16, 128),
        bf(128, 16, 128),
        bf(512, 512),
        bf(512, 512),
        bf(128, 16, 128),
        bf(128, 16, 128),
        bf(128, 16, 128),
        bf(128, 16, 128),
        bf(640, 2048),
        fl(512, 128),
        fl(64, 8, 128),
        fl(3, 8, 128),
        fl(512, 128),
        fl(64, 8, 128),
        fl(3, 8, 128),
        pltpu.SemaphoreType.DMA((6,)),
        pltpu.SemaphoreType.DMA((2,)),
        pltpu.SemaphoreType.DMA((12,)),
        pltpu.SemaphoreType.DMA((12,)),
    ]
    shapes = [
        jax.ShapeDtypeStruct((CELLS, CH), BF16),
        jax.ShapeDtypeStruct((CELLS, CH), BF16),
        jax.ShapeDtypeStruct((1, CH), F32),
        jax.ShapeDtypeStruct((CH, 640), F32),
        jax.ShapeDtypeStruct((1, CH), F32),
        jax.ShapeDtypeStruct((CH, CH), F32),
    ]
    params = (in_gain.reshape(1, CH), w_in, out_gain.reshape(1, CH), w_out)
    sums_shape = jax.ShapeDtypeStruct((512, 128), F32)
    results = pl.pallas_call(
        kernel,
        out_shape=shapes[:2] + [sums_shape] * 2,
        in_specs=[hbm] * 6,
        out_specs=[hbm] * 4,
        scratch_shapes=scratch,
        compiler_params=pltpu.CompilerParams(
            collective_id=0, has_side_effects=True, vmem_limit_bytes=VMEM_BYTES
        ),
        name="triangle_update",
    )(pair.reshape(CELLS, CH), cotangent.reshape(CELLS, CH), *params)
    pair_next, pair_back, in_gain_grad, w_in_grad, out_gain_grad, w_out_grad = pl.pallas_call(
        deliver,
        out_shape=shapes,
        in_specs=[hbm] * 8,
        out_specs=[hbm] * 6,
        scratch_shapes=[
            bf(CELLS, CH),
            bf(CELLS, CH),
            fl(512, 128),
            fl(512, 128),
            fl(1, CH),
            bf(CH, 640),
            fl(1, CH),
            bf(CH, CH),
            fl(1, CH),
            fl(CH, 640),
            fl(1, CH),
            fl(CH, CH),
            pltpu.SemaphoreType.DMA((8,)),
            pltpu.SemaphoreType.DMA((6,)),
        ],
        compiler_params=pltpu.CompilerParams(vmem_limit_bytes=VMEM_BYTES),
        name="deliver",
    )(*results, *params)
    return (
        pair_next.reshape(64, 32, CH),
        pair_back.reshape(64, 32, CH),
        in_gain_grad.reshape(CH),
        w_in_grad,
        out_gain_grad.reshape(CH),
        w_out_grad,
    )


def solution(mesh):
    in_specs = (P("row", "col", None), P("row", "col", None), P(), P(), P(), P())
    out_specs = (P("row", "col", None), P("row", "col", None), P(), P(), P(), P())
    return jax.shard_map(
        on_device, mesh=mesh, in_specs=in_specs, out_specs=out_specs, check_vma=False
    )
```
